32 devices in a mesh: lat: 2 (over x), lon: 8 (over z, core), head: 2 (over y).
Axes of the slice: x: 2, y: 2, z: 4, core: 2. Of those that a mesh axis runs over, the one named last changes fastest.
Arguments:
- queries: bfloat16 [16, 384, 1024], P('lat', ('lon', 'head')), may hold values from -28 to 28
- keys_in: bfloat16 [16, 384, 1024], P('lat', ('lon', 'head')), may hold values from -28 to 28
- values: bfloat16 [16, 384, 1024], P('lat', ('lon', 'head')), may hold values from -6 to 6
- grad_out: bfloat16 [16, 384, 1024], P('lat', ('lon', 'head')), may hold values from -6 to 6
Outputs:
- attended: bfloat16 [16, 384, 1024], P('lat', ('lon', 'head'))
- grad_query: bfloat16 [16, 384, 1024], P('lat', ('lon', 'head'))
- grad_key: bfloat16 [16, 384, 1024], P('lat', ('lon', 'head'))
- grad_value: bfloat16 [16, 384, 1024], P('lat', ('lon', 'head'))
The draws below stay inside these ranges and needn't reach their ends.
All inputs are finite; a program needn't handle non-finite values.
Results may differ from the reference program's by a relative error of at most 0.02.
Values may be sent and summed in bfloat16 or wider, within the bound.
A program may use at most 128 MiB of HBM per device.

```python
import jax
import jax.numpy as jnp
from jax import lax

HEADS = 16
HD = 64
WIN = 13
RAD = 6
NLAT = 16
NLON = 384


def draw_queries(key, part):
    result = jnp.clip(jax.random.normal(jax.random.fold_in(key, 11), (NLAT, NLON, HEADS, HD), jnp.float32), -6.0, 6.0)
    return result.reshape(NLAT, NLON, HEADS * HD).astype(jnp.bfloat16)


def draw_keys_in(key, part):
    result = jnp.clip(jax.random.normal(jax.random.fold_in(key, 12), (NLAT, NLON, HEADS, HD), jnp.float32), -6.0, 6.0)
    return result.reshape(NLAT, NLON, HEADS * HD).astype(jnp.bfloat16)


def levels(stream_key, shape, shards, smallest, largest):
    loudness = 1.0
    for position, shards_of in shards:
        heights = jax.random.uniform(jax.random.fold_in(jax.random.fold_in(stream_key, 6), position), (shards_of,), jnp.float32, smallest / len(shards), largest / len(shards))
        loudness = loudness * jnp.repeat(jnp.exp(heights), shape[position] // shards_of).reshape((-1,) + (1,) * (len(shape) - 1 - position))
    return loudness


def bell_draw(stream_key, dims, deviation, limit, cuts=(), held_as=jnp.bfloat16):
    values = jax.random.normal(stream_key, dims, jnp.float32) * deviation
    if len(cuts) > 0:
        values = levels(stream_key, dims, cuts, -0.22, 0.18) * values
    return jnp.clip(values, min=-limit, max=limit).astype(held_as)


def setup_inputs(seed: int = 0) -> dict:
    seeds = jax.random.split(jax.random.key(seed), 5)
    return {
        "queries": draw_queries(jax.random.fold_in(seeds[4], 71), 0),
        "keys_in": draw_keys_in(jax.random.fold_in(seeds[4], 71), 0),
        "values": bell_draw(seeds[2], (NLAT, NLON, HEADS * HD), 1.0, 6.0, ((0, 2), (1, 16))),
        "grad_out": bell_draw(seeds[3], (NLAT, NLON, HEADS * HD), 1.0, 6.0, ((0, 2), (1, 16))),
    }


def extend(plane):
    padded = jnp.pad(plane, ((RAD, RAD), (0, 0), (0, 0)))
    return jnp.concatenate([padded[:, NLON - RAD:], padded, padded[:, :RAD]], axis=1)


def shifted(padded, offset):
    return lax.dynamic_slice(padded, (offset // WIN, offset % WIN, jnp.int32(0)), (NLAT, NLON, HD))


def fold_back(padded):
    interior = padded[RAD:RAD + NLAT]
    middle = interior[:, RAD:RAD + NLON]
    middle = middle.at[:, NLON - RAD:].add(interior[:, :RAD])
    middle = middle.at[:, :RAD].add(interior[:, NLON + RAD:])
    return middle


def head_pass(inputs):
    query_plane, key_plane, value_plane, grad_plane = inputs
    score_scale = HD ** -0.5
    query_f = query_plane.astype(jnp.float32)
    grad_f = grad_plane.astype(jnp.float32)
    key_pad = extend(key_plane.astype(jnp.float32))
    value_pad = extend(value_plane.astype(jnp.float32))
    offsets = jnp.arange(WIN * WIN, dtype=jnp.int32)
    lat_rows = jnp.arange(NLAT, dtype=jnp.int32)

    def score_at(offset):
        lat_key = lat_rows + offset // WIN - RAD
        inside = ((lat_key >= 0) & (lat_key < NLAT))[:, None]
        raw_score = jnp.sum(query_f * shifted(key_pad, offset), axis=-1) * score_scale
        return jnp.where(inside, raw_score, -jnp.inf)

    scores = lax.map(score_at, offsets)
    row_max = jnp.max(scores, axis=0)
    log_total = row_max + jnp.log(jnp.sum(jnp.exp(scores - row_max), axis=0))
    probabilities = jnp.exp(scores - log_total).astype(jnp.bfloat16)
    zeros_plane = jnp.zeros((NLAT, NLON, HD), jnp.float32)

    def add_value(running, items):
        offset, weight = items
        return running + weight.astype(jnp.float32)[..., None] * shifted(value_pad, offset), None

    attended = lax.scan(add_value, zeros_plane, (offsets, probabilities))[0].astype(jnp.bfloat16)
    row_dot = jnp.sum(grad_f * attended.astype(jnp.float32), axis=-1)

    def slope_at(items):
        offset, weight = items
        along = jnp.sum(grad_f * shifted(value_pad, offset), axis=-1)
        return (weight.astype(jnp.float32) * (along - row_dot)).astype(jnp.bfloat16)

    slopes = lax.map(slope_at, (offsets, probabilities))

    def add_query(running, items):
        offset, slope = items
        return running + slope.astype(jnp.float32)[..., None] * shifted(key_pad, offset), None

    grad_query = (lax.scan(add_query, zeros_plane, (offsets, slopes))[0] * score_scale).astype(jnp.bfloat16)
    pad_zeros = jnp.zeros((NLAT + 2 * RAD, NLON + 2 * RAD, 2 * HD), jnp.float32)

    def add_keys(running, items):
        offset, slope, weight = items
        term = jnp.concatenate([slope.astype(jnp.float32)[..., None] * query_f, weight.astype(jnp.float32)[..., None] * grad_f], axis=-1)
        start = (offset // WIN, offset % WIN, jnp.int32(0))
        current = lax.dynamic_slice(running, start, (NLAT, NLON, 2 * HD))
        return lax.dynamic_update_slice(running, current + term, start), None

    key_sums = fold_back(lax.scan(add_keys, pad_zeros, (offsets, slopes, probabilities))[0])
    grad_key = (key_sums[..., :HD] * score_scale).astype(jnp.bfloat16)
    grad_value = key_sums[..., HD:].astype(jnp.bfloat16)
    return attended, grad_query, grad_key, grad_value


def reference(queries, keys_in, values, grad_out):
    def by_head(stacked):
        return stacked.reshape(NLAT, NLON, HEADS, HD).transpose(2, 0, 1, 3)

    def to_grid(stacked):
        return stacked.transpose(1, 2, 0, 3).reshape(NLAT, NLON, HEADS * HD)

    results = lax.map(head_pass, (by_head(queries), by_head(keys_in), by_head(values), by_head(grad_out)))
    return (to_grid(results[0]), to_grid(results[1]), to_grid(results[2]), to_grid(results[3]))
```

```python
import functools

import jax
import jax.numpy as jnp
import numpy as np
from jax import lax
from jax.experimental import pallas as pl
from jax.experimental.pallas import tpu as pltpu
from jax.sharding import PartitionSpec as P

HD = 64
RAD = 6
LANES = 256
MASKED = -1e30
MESH = pl.DeviceIdType.MESH


def rounded_up(size, step):
    return -(-size // step) * step


def tables(rows, cols, slots):
    tokens, strip = rows * cols, RAD * cols
    edge = rows * RAD
    corner = rounded_up(RAD * RAD, 16)
    lead = corner - RAD * RAD
    region = 2 * corner - 16
    count = rounded_up(tokens + 2 * edge + slots * (strip + region), 128)
    where = np.zeros((count, 128), np.float32)

    def put(at, row, col, slot=None):
        where[at, 0], where[at, 1], where[at, 4] = row, col, 1
        if slot is not None:
            where[at, 2 + slot] = 1

    for i in range(tokens):
        put(i, i // cols, i % cols)
    for i in range(edge):
        put(tokens + i, i // RAD, i % RAD - RAD)
        put(tokens + edge + i, i // RAD, cols + i % RAD)
    base = tokens + 2 * edge
    for slot in range(slots):
        for i in range(strip):
            put(base + slot * strip + i, i // cols, i % cols, slot)
        start = base + slots * strip + slot * region
        for i in range(RAD * RAD):
            put(start + i, i // RAD, i % RAD - RAD, slot)
            put(start + region - RAD * RAD + i, i // RAD, cols + i % RAD, slot)
    pick_edge = np.zeros((2 * edge, tokens), np.float32)
    for i in range(edge):
        pick_edge[i, (i // RAD) * cols + cols - RAD + i % RAD] = 1
        pick_edge[edge + i, (i // RAD) * cols + i % RAD] = 1
    pick_corner = np.zeros((2 * corner, strip), np.float32)
    for i in range(RAD * RAD):
        pick_corner[i, (i // RAD) * cols + cols - RAD + i % RAD] = 1
        pick_corner[corner + lead + i, (i // RAD) * cols + i % RAD] = 1
    heads = LANES // HD
    place = np.zeros((8, heads * tokens), np.float32)
    for i in range(tokens):
        place[0, i::tokens] = i // cols
        place[1, i::tokens] = i % cols
    return where, place, pick_edge, pick_corner


def dot(a, b, a_dim=1, b_dim=0):
    return lax.dot_general(a, b, (((a_dim,), (b_dim,)), ((), ())), preferred_element_type=jnp.float32)


def kernel(
    dims, q_ref, k_ref, v_ref, g_ref, where_ref, place_ref, edge_ref, edge_t_ref, corner_ref, corner_t_ref,
    att_ref, dq_ref, dk_ref, dv_ref,
    bias, keys, got_lat, put_edge, got_edge, put_corner, got_corner, put_side, got_side, put_lat, got_back,
    own, lat_sum, lat_s, lat_r, edge_s, edge_r, corner_s, corner_r, side_s, side_r, back_s, back_r,
):
    rows, cols, slots, n_lat, n_lon, n_head, chunks = dims
    tokens, strip, edge = rows * cols, RAD * cols, rows * RAD
    corner = rounded_up(RAD * RAD, 16)
    region = 2 * corner - 16
    used = tokens + 2 * edge + slots * (strip + region)
    count = keys.shape[0]
    heads = LANES // HD
    lat, lon, head = lax.axis_index("lat"), lax.axis_index("lon"), lax.axis_index("head")
    column = lon * n_head + head
    ring = n_lon * n_head

    def beside(step):
        c = lax.rem(column + step + ring, ring)
        return (lat, c // n_head, lax.rem(c, n_head))

    right, left = beside(1), beside(-1)
    if slots == 1:
        partners = [(1 - lat, lon, head)]
        first_row = [(1 - lat) * ((rows - RAD) * cols)]
        strip_row = [rows - lat * (rows + RAD)]
        far_slot = [0]
    else:
        partners = [(lax.rem(lat + n_lat - 1, n_lat), lon, head), (lax.rem(lat + 1, n_lat), lon, head)]
        first_row = [0, (rows - RAD) * cols]
        strip_row = [-RAD, rows]
        far_slot = [1, 0]

    def strip_of(slot):
        start = first_row[slot]
        if not isinstance(start, int):
            start = pl.multiple_of(start, 16)
        return pl.ds(start, strip)

    def lanes_of(g):
        return pl.ds(pl.multiple_of(g * LANES, LANES), LANES)

    def remote(src, dst, s, r, device):
        return pltpu.make_async_remote_copy(
            src_ref=src, dst_ref=dst, send_sem=s, recv_sem=r, device_id=device, device_id_type=MESH
        )

    def lat_copies(g):
        made = []
        for slot in range(slots):
            for half, ref in enumerate((k_ref, v_ref)):
                made.append(
                    remote(
                        ref.at[strip_of(slot), lanes_of(g)],
                        got_lat.at[g, far_slot[slot], :, pl.ds(half * LANES, LANES)],
                        lat_s.at[g, 2 * slot + half], lat_r.at[g, 2 * far_slot[slot] + half], partners[slot],
                    )
                )
        return made

    def edge_copies(g):
        return [
            remote(put_edge.at[g, side], got_edge.at[g, side], edge_s.at[g, side], edge_r.at[g, side], device)
            for side, device in enumerate((right, left))
        ]

    def corner_copies(g):
        return [
            remote(
                put_corner.at[g, 2 * slot + side], got_corner.at[g, 2 * slot + side],
                corner_s.at[g, 2 * slot + side], corner_r.at[g, 2 * slot + side], device,
            )
            for slot in range(slots)
            for side, device in enumerate((right, left))
        ]

    def side_copies(g):
        return [
            remote(put_side.at[g, side], got_side.at[g, side], side_s.at[g, side], side_r.at[g, side], device)
            for side, device in enumerate((left, right))
        ]

    def back_copies(g):
        return [
            remote(
                put_lat.at[g, slot], got_back.at[g, far_slot[slot]],
                back_s.at[g, slot], back_r.at[g, far_slot[slot]], partners[slot],
            )
            for slot in range(slots)
        ]

    def send_edges(g):
        for half, ref in enumerate((k_ref, v_ref)):
            picked = dot(edge_ref[...], ref[:, lanes_of(g)]).astype(jnp.bfloat16)
            at = pl.ds(half * LANES, LANES)
            put_edge[g, 0, :, at] = picked[:edge]
            put_edge[g, 1, :, at] = picked[edge:]
        for copy in edge_copies(g):
            copy.start()

    barrier = pltpu.get_barrier_semaphore()
    for device in [left, right] + partners:
        pl.semaphore_signal(barrier, inc=1, device_id=device, device_id_type=MESH)
    pl.semaphore_wait(barrier, 2 + slots)

    def start_lat(g, carry):
        for copy in lat_copies(g):
            copy.start()
        return carry

    lax.fori_loop(0, chunks, start_lat, 0)
    send_edges(0)

    info = where_ref[...]
    key_row, key_col = info[:, 0:1], info[:, 1:2]
    for slot in range(slots):
        shift = jnp.asarray(strip_row[slot], jnp.int32).astype(jnp.float32)
        key_row = key_row + info[:, 2 + slot : 3 + slot] * shift
    lat_row = key_row + (lat * rows).astype(jnp.float32)
    valid = (info[:, 4:5] > 0.5) & (lat_row >= 0.0) & (lat_row <= float(rows * n_lat - 1))
    key_row = jnp.where(valid, key_row, 1000.0)
    near = (jnp.abs(key_row - place_ref[0:1, :]) <= RAD) & (jnp.abs(key_col - place_ref[1:2, :]) <= RAD)
    bias[...] = jnp.where(near, 0.0, MASKED)
    if count > used:
        keys[pl.ds(used, count - used), :] = jnp.zeros((count - used, 2 * LANES), jnp.bfloat16)

    lane_head = lax.broadcasted_iota(jnp.int32, (tokens, LANES), 1) // HD
    ones = [jnp.where(lane_head == h, 1.0, 0.0).astype(jnp.bfloat16) for h in range(heads)]

    def by_head(block):
        return jnp.concatenate([block * one for one in ones], axis=0)

    def from_heads(stacked):
        total = stacked[:tokens] * ones[0]
        for h in range(1, heads):
            total = total + stacked[h * tokens : (h + 1) * tokens] * ones[h]
        return total

    def spread_corners(g):
        for copy in lat_copies(g):
            copy.wait_recv()
        for slot in range(slots):
            picked = dot(corner_ref[...], got_lat[g, slot]).astype(jnp.bfloat16)
            put_corner[g, 2 * slot] = picked[:corner]
            put_corner[g, 2 * slot + 1] = picked[corner:]
        for copy in corner_copies(g):
            copy.start()

        @pl.when(g + 1 < chunks)
        def _():
            send_edges(g + 1)

    def attend(g):
        lanes = lanes_of(g)
        for copy in edge_copies(g) + corner_copies(g):
            copy.wait_recv()
        keys[pl.ds(0, tokens), pl.ds(0, LANES)] = k_ref[:, lanes]
        keys[pl.ds(0, tokens), pl.ds(LANES, LANES)] = v_ref[:, lanes]
        for side in range(2):
            keys[pl.ds(tokens + side * edge, edge), :] = got_edge[g, side]
        base = tokens + 2 * edge
        for slot in range(slots):
            keys[pl.ds(base + slot * strip, strip), :] = got_lat[g, slot]
            start = base + slots * strip + slot * region
            low, high = got_corner[g, 2 * slot], got_corner[g, 2 * slot + 1]
            keys[pl.ds(start, corner - 16), :] = low[: corner - 16]
            keys[pl.ds(start + corner - 16, 16), :] = low[corner - 16 :] + high[:16]
            keys[pl.ds(start + corner, corner - 16), :] = high[16:]
        key_block = keys[:, pl.ds(0, LANES)]
        value_block = keys[:, pl.ds(LANES, LANES)]
        query_block = by_head(q_ref[:, lanes])
        grad_block = by_head(g_ref[:, lanes])
        scale = HD ** -0.5
        scores = dot(key_block, query_block, 1, 1) * scale + bias[...]
        weights = jnp.exp(scores - jnp.max(scores, axis=0, keepdims=True))
        weights = weights * (1.0 / jnp.sum(weights, axis=0, keepdims=True))
        probabilities = weights.astype(jnp.bfloat16)
        value_term = dot(probabilities, grad_block)
        attended = dot(value_block.T, probabilities).astype(jnp.bfloat16)
        att_ref[:, lanes] = from_heads(attended.T)
        along = dot(value_block, grad_block, 1, 1)
        weights = probabilities.astype(jnp.float32)
        row_dot = jnp.sum(weights * along, axis=0, keepdims=True)
        slopes = (weights * (along - row_dot)).astype(jnp.bfloat16)
        key_term = dot(slopes, query_block) * scale
        grad_query = (dot(key_block.T, slopes) * scale).astype(jnp.bfloat16)
        dq_ref[:, lanes] = from_heads(grad_query.T)
        for half, term in enumerate((key_term, value_term)):
            at = pl.ds(half * LANES, LANES)
            own[g, :, at] = term[:tokens]
            for side in range(2):
                put_side[g, side, pl.ds(0, edge), at] = term[
                    tokens + side * edge : tokens + (side + 1) * edge
                ].astype(jnp.bfloat16)
            for slot in range(slots):
                lat_sum[g, slot, :, at] = term[base + slot * strip : base + (slot + 1) * strip]
                start = base + slots * strip + slot * region
                for side in range(2):
                    first = start + side * (corner - 16)
                    put_side[g, side, pl.ds(edge + slot * corner, corner), at] = term[
                        first : first + corner
                    ].astype(jnp.bfloat16)
        for copy in side_copies(g):
            copy.start()

    def gather_sides(g):
        for copy in side_copies(g):
            copy.wait_recv()
        low, high = got_side[g, 0], got_side[g, 1]
        own[g] += dot(edge_t_ref[...], jnp.concatenate([low[:edge], high[:edge]], axis=0))
        for slot in range(slots):
            at = edge + slot * corner
            corners = jnp.concatenate([low[at : at + corner], high[at : at + corner]], axis=0)
            total = lat_sum[g, slot] + dot(corner_t_ref[...], corners)
            put_lat[g, slot] = total.astype(jnp.bfloat16)
        for copy in back_copies(g):
            copy.start()

    def finish(g):
        for copy in back_copies(g):
            copy.wait_recv()
        for slot in range(slots):
            own[g, strip_of(slot), :] += got_back[g, slot].astype(jnp.float32)
        dk_ref[:, lanes_of(g)] = own[g, :, pl.ds(0, LANES)].astype(jnp.bfloat16)
        dv_ref[:, lanes_of(g)] = own[g, :, pl.ds(LANES, LANES)].astype(jnp.bfloat16)

    def step(t, carry):
        for delay, stage in enumerate((spread_corners, attend, gather_sides, finish)):
            pl.when((t >= delay) & (t < chunks + delay))(functools.partial(stage, t - delay))
        return carry

    lax.fori_loop(0, chunks + 3, step, 0)

    def drain(g, carry):
        for copy in lat_copies(g) + edge_copies(g) + corner_copies(g) + side_copies(g) + back_copies(g):
            copy.wait_send()
        return carry

    lax.fori_loop(0, chunks, drain, 0)


def local(sizes, queries, keys_in, values, grad_out):
    n_lat, n_lon, n_head = sizes
    rows, cols, features = queries.shape
    slots = 1 if n_lat == 2 else 2
    chunks = features // LANES
    tokens, strip, edge = rows * cols, RAD * cols, rows * RAD
    corner = rounded_up(RAD * RAD, 16)
    side = edge + slots * corner
    where, place, pick_edge, pick_corner = tables(rows, cols, slots)
    count = where.shape[0]
    wide = 2 * LANES
    bf16, f32 = jnp.bfloat16, jnp.float32
    vmem = pl.BlockSpec(memory_space=pltpu.VMEM)
    flops = 12 * count * tokens * (LANES // HD) * LANES * chunks
    sems = [(chunks, 2 * slots)] * 2 + [(chunks, 2)] * 2 + [(chunks, 2 * slots)] * 2 + [(chunks, 2)] * 2
    sems += [(chunks, slots)] * 2
    out = pl.pallas_call(
        functools.partial(kernel, (rows, cols, slots, n_lat, n_lon, n_head, chunks)),
        out_shape=[jax.ShapeDtypeStruct((tokens, features), bf16)] * 4,
        in_specs=[vmem] * 10,
        out_specs=[vmem] * 4,
        scratch_shapes=[
            pltpu.VMEM((count, place.shape[1]), f32),
            pltpu.VMEM((count, wide), bf16),
            pltpu.VMEM((chunks, slots, strip, wide), bf16),
            pltpu.VMEM((chunks, 2, edge, wide), bf16),
            pltpu.VMEM((chunks, 2, edge, wide), bf16),
            pltpu.VMEM((chunks, 2 * slots, corner, wide), bf16),
            pltpu.VMEM((chunks, 2 * slots, corner, wide), bf16),
            pltpu.VMEM((chunks, 2, side, wide), bf16),
            pltpu.VMEM((chunks, 2, side, wide), bf16),
            pltpu.VMEM((chunks, slots, strip, wide), bf16),
            pltpu.VMEM((chunks, slots, strip, wide), bf16),
            pltpu.VMEM((chunks, tokens, wide), f32),
            pltpu.VMEM((chunks, slots, strip, wide), f32),
        ]
        + [pltpu.SemaphoreType.DMA(shape) for shape in sems],
        compiler_params=pltpu.CompilerParams(
            collective_id=0, has_side_effects=True, vmem_limit_bytes=50 * 1024 * 1024
        ),
        cost_estimate=pl.CostEstimate(flops=flops, bytes_accessed=8 * tokens * features * 2, transcendentals=0),
    )(
        *(x.reshape(tokens, features) for x in (queries, keys_in, values, grad_out)),
        jnp.asarray(where), jnp.asarray(place),
        jnp.asarray(pick_edge, bf16), jnp.asarray(np.ascontiguousarray(pick_edge.T), bf16),
        jnp.asarray(pick_corner, bf16), jnp.asarray(np.ascontiguousarray(pick_corner.T), bf16),
    )
    return tuple(x.reshape(rows, cols, features) for x in out)


def solution(mesh):
    spec = P("lat", ("lon", "head"), None)
    sizes = tuple(mesh.shape[axis] for axis in ("lat", "lon", "head"))
    return jax.shard_map(
        functools.partial(local, sizes), mesh=mesh, in_specs=(spec,) * 4, out_specs=(spec,) * 4, check_vma=False
    )
```

```python
import functools

import jax
import jax.numpy as jnp
from jax import lax
from jax.experimental import pallas as pl
from jax.experimental.pallas import tpu as pltpu
from jax.sharding import PartitionSpec as P

HD = 64
RAD = 6
LANES = 256
MASKED = -1e30
MESH = pl.DeviceIdType.MESH


def rounded_up(size, step):
    return -(-size // step) * step


def floor_div(i, n):
    return jnp.floor((i + 0.5) * (1.0 / n))


def counted(shape, dim):
    return lax.broadcasted_iota(jnp.int32, shape, dim).astype(jnp.float32)


def edge_token(i, count, cols):
    first = jnp.where(i < count, cols - RAD, 0.0)
    i = jnp.where(i < count, i, i - count)
    row = floor_div(i, RAD)
    return row * cols + (i - row * RAD) + first


def corner_token(i, corner, cols):
    size = RAD * RAD
    lead = corner - size
    token = edge_token(jnp.where(i < corner, i, i - corner - lead + size), size, cols)
    real = (i < size) | (i >= corner + lead)
    return jnp.where(real, token, -1.0)


def key_places(count, rows, cols, strip_row):
    slots = len(strip_row)
    tokens, strip, edge = rows * cols, RAD * cols, rows * RAD
    corner = rounded_up(RAD * RAD, 16)
    region = 2 * corner - 16
    i = counted((count, 1), 0)
    row = floor_div(i, cols)
    col = i - row * cols
    real = jnp.where(i < tokens + 2 * edge + slots * (strip + region), 1.0, 0.0)
    for side in range(2):
        at = i - (tokens + side * edge)
        here = (at >= 0) & (at < edge)
        r = floor_div(at, RAD)
        row = jnp.where(here, r, row)
        col = jnp.where(here, at - r * RAD + (cols if side else -RAD), col)
    base = tokens + 2 * edge
    for slot in range(slots):
        top = jnp.asarray(strip_row[slot], jnp.int32).astype(jnp.float32)
        at = i - (base + slot * strip)
        here = (at >= 0) & (at < strip)
        r = floor_div(at, cols)
        row = jnp.where(here, r + top, row)
        col = jnp.where(here, at - r * cols, col)
        for side in range(2):
            start = base + slots * strip + slot * region
            at = i - (start + side * (region - RAD * RAD))
            here = (at >= 0) & (at < RAD * RAD)
            r = floor_div(at, RAD)
            row = jnp.where(here, r + top, row)
            col = jnp.where(here, at - r * RAD + (cols if side else -RAD), col)
        at = i - (base + slots * strip + slot * region)
        real = jnp.where((at >= RAD * RAD) & (at < region - RAD * RAD), 0.0, real)
    return row, col, real > 0.5


def dot(a, b, a_dim=1, b_dim=0):
    return lax.dot_general(a, b, (((a_dim,), (b_dim,)), ((), ())), preferred_element_type=jnp.float32)


def kernel(
    dims, q_hbm, k_hbm, v_hbm, g_hbm, att_hbm, dq_hbm, dk_hbm, dv_hbm,
    att_ref, dq_ref, dk_ref, dv_ref, q_ref, k_ref, v_ref, g_ref, edge_ref, edge_t_ref, corner_ref, corner_t_ref, bias, keys, got_lat, put_edge, got_edge, put_corner, got_corner, put_side, got_side, put_lat, got_back,
    own, lat_sum, load_sem, save_sem, lat_s, lat_r, edge_s, edge_r, corner_s, corner_r, side_s, side_r, back_s, back_r,
):
    rows, cols, slots, n_lat, n_lon, n_head, chunks = dims
    tokens, strip, edge = rows * cols, RAD * cols, rows * RAD
    corner = rounded_up(RAD * RAD, 16)
    region = 2 * corner - 16
    used = tokens + 2 * edge + slots * (strip + region)
    count = keys.shape[0]
    heads = LANES // HD
    lat, lon, head = lax.axis_index("lat"), lax.axis_index("lon"), lax.axis_index("head")
    column = lon * n_head + head
    ring = n_lon * n_head

    def beside(step):
        c = lax.rem(column + step + ring, ring)
        return (lat, c // n_head, lax.rem(c, n_head))

    right, left = beside(1), beside(-1)
    if slots == 1:
        partners = [(1 - lat, lon, head)]
        first_row = [(1 - lat) * ((rows - RAD) * cols)]
        strip_row = [rows - lat * (rows + RAD)]
        far_slot = [0]
    else:
        partners = [(lax.rem(lat + n_lat - 1, n_lat), lon, head), (lax.rem(lat + 1, n_lat), lon, head)]
        first_row = [0, (rows - RAD) * cols]
        strip_row = [-RAD, rows]
        far_slot = [1, 0]

    def strip_of(slot):
        start = first_row[slot]
        if not isinstance(start, int):
            start = pl.multiple_of(start, 16)
        return pl.ds(start, strip)

    def lanes_of(g):
        return pl.ds(pl.multiple_of(g * LANES, LANES), LANES)

    def remote(src, dst, s, r, device):
        return pltpu.make_async_remote_copy(
            src_ref=src, dst_ref=dst, send_sem=s, recv_sem=r, device_id=device, device_id_type=MESH
        )

    def lat_copies(g):
        made = []
        for slot in range(slots):
            for half, ref in enumerate((k_hbm, v_hbm)):
                made.append(
                    remote(
                        ref.at[strip_of(slot), lanes_of(g)],
                        got_lat.at[g, far_slot[slot], :, pl.ds(half * LANES, LANES)],
                        lat_s.at[g, 2 * slot + half], lat_r.at[g, 2 * far_slot[slot] + half], partners[slot],
                    )
                )
        return made

    def edge_copies(g):
        return [
            remote(put_edge.at[g, side], got_edge.at[g, side], edge_s.at[g, side], edge_r.at[g, side], device)
            for side, device in enumerate((right, left))
        ]

    def corner_copies(g):
        return [
            remote(
                put_corner.at[g, 2 * slot + side], got_corner.at[g, 2 * slot + side],
                corner_s.at[g, 2 * slot + side], corner_r.at[g, 2 * slot + side], device,
            )
            for slot in range(slots)
            for side, device in enumerate((right, left))
        ]

    def side_copies(g):
        return [
            remote(put_side.at[g, side], got_side.at[g, side], side_s.at[g, side], side_r.at[g, side], device)
            for side, device in enumerate((left, right))
        ]

    def back_copies(g):
        return [
            remote(
                put_lat.at[g, slot], got_back.at[g, far_slot[slot]],
                back_s.at[g, slot], back_r.at[g, far_slot[slot]], partners[slot],
            )
            for slot in range(slots)
        ]

    def saves(g, first):
        pairs = ((att_ref, att_hbm), (dq_ref, dq_hbm), (dk_ref, dk_hbm), (dv_ref, dv_hbm))
        return [
            pltpu.make_async_copy(src.at[:, lanes_of(g)], dst.at[:, lanes_of(g)], save_sem.at[g, first + n])
            for n, (src, dst) in enumerate(pairs[first : first + 2])
        ]

    def send_edges(g):
        for half, ref in enumerate((k_ref, v_ref)):
            picked = dot(edge_ref[...], ref[:, lanes_of(g)]).astype(jnp.bfloat16)
            at = pl.ds(half * LANES, LANES)
            put_edge[g, 0, :, at] = picked[:edge]
            put_edge[g, 1, :, at] = picked[edge:]
        for copy in edge_copies(g):
            copy.start()

    loads = [
        pltpu.make_async_copy(src, dst, load_sem.at[n])
        for n, (src, dst) in enumerate(((k_hbm, k_ref), (v_hbm, v_ref), (q_hbm, q_ref), (g_hbm, g_ref)))
    ]
    for load in loads:
        load.start()
    barrier = pltpu.get_barrier_semaphore()
    for device in [left, right] + partners:
        pl.semaphore_signal(barrier, inc=1, device_id=device, device_id_type=MESH)
    pl.semaphore_wait(barrier, 2 + slots)

    def start_lat(g, carry):
        for copy in lat_copies(g):
            copy.start()
        return carry

    lax.fori_loop(0, chunks, start_lat, 0)

    def one_hot(token, place):
        return jnp.where(token == place, 1.0, 0.0).astype(jnp.bfloat16)

    n = 2 * edge
    edge_ref[...] = one_hot(edge_token(counted((n, 1), 0), edge, cols), counted((n, tokens), 1))
    loads[0].wait()
    loads[1].wait()
    send_edges(0)
    edge_t_ref[...] = one_hot(edge_token(counted((1, n), 1), edge, cols), counted((tokens, n), 0))
    n = 2 * corner
    corner_ref[...] = one_hot(corner_token(counted((n, 1), 0), corner, cols), counted((n, strip), 1))
    corner_t_ref[...] = one_hot(corner_token(counted((1, n), 1), corner, cols), counted((strip, n), 0))
    key_row, key_col, real = key_places(count, rows, cols, strip_row)
    lat_row = key_row + (lat * rows).astype(jnp.float32)
    valid = real & (lat_row >= 0.0) & (lat_row <= float(rows * n_lat - 1))
    key_row = jnp.where(valid, key_row, 1000.0)
    place = counted((1, heads * tokens), 1)
    place = place - floor_div(place, tokens) * tokens
    place_row = floor_div(place, cols)
    place_col = place - place_row * cols
    near = (jnp.abs(key_row - place_row) <= RAD) & (jnp.abs(key_col - place_col) <= RAD)
    bias[...] = jnp.where(near, 0.0, MASKED)
    if count > used:
        keys[pl.ds(used, count - used), :] = jnp.zeros((count - used, 2 * LANES), jnp.bfloat16)

    loads[2].wait()
    loads[3].wait()
    lane_head = lax.broadcasted_iota(jnp.int32, (tokens, LANES), 1) // HD
    ones = [jnp.where(lane_head == h, 1.0, 0.0).astype(jnp.bfloat16) for h in range(heads)]

    def by_head(block):
        return jnp.concatenate([block * one for one in ones], axis=0)

    def from_heads(stacked):
        total = stacked[:tokens] * ones[0]
        for h in range(1, heads):
            total = total + stacked[h * tokens : (h + 1) * tokens] * ones[h]
        return total

    def spread_corners(g):
        for copy in lat_copies(g):
            copy.wait_recv()
        for slot in range(slots):
            picked = dot(corner_ref[...], got_lat[g, slot]).astype(jnp.bfloat16)
            put_corner[g, 2 * slot] = picked[:corner]
            put_corner[g, 2 * slot + 1] = picked[corner:]
        for copy in corner_copies(g):
            copy.start()

        @pl.when(g + 1 < chunks)
        def _():
            send_edges(g + 1)

    def attend(g):
        lanes = lanes_of(g)
        for copy in edge_copies(g) + corner_copies(g):
            copy.wait_recv()
        keys[pl.ds(0, tokens), pl.ds(0, LANES)] = k_ref[:, lanes]
        keys[pl.ds(0, tokens), pl.ds(LANES, LANES)] = v_ref[:, lanes]
        for side in range(2):
            keys[pl.ds(tokens + side * edge, edge), :] = got_edge[g, side]
        base = tokens + 2 * edge
        for slot in range(slots):
            keys[pl.ds(base + slot * strip, strip), :] = got_lat[g, slot]
            start = base + slots * strip + slot * region
            low, high = got_corner[g, 2 * slot], got_corner[g, 2 * slot + 1]
            keys[pl.ds(start, corner - 16), :] = low[: corner - 16]
            keys[pl.ds(start + corner - 16, 16), :] = low[corner - 16 :] + high[:16]
            keys[pl.ds(start + corner, corner - 16), :] = high[16:]
        key_block = keys[:, pl.ds(0, LANES)]
        value_block = keys[:, pl.ds(LANES, LANES)]
        query_block = by_head(q_ref[:, lanes])
        grad_block = by_head(g_ref[:, lanes])
        scale = HD ** -0.5
        scores = dot(key_block, query_block, 1, 1) * scale + bias[...]
        weights = jnp.exp(scores - jnp.max(scores, axis=0, keepdims=True))
        weights = weights * (1.0 / jnp.sum(weights, axis=0, keepdims=True))
        probabilities = weights.astype(jnp.bfloat16)
        value_term = dot(probabilities, grad_block)
        along = dot(value_block, grad_block, 1, 1)
        weights = probabilities.astype(jnp.float32)
        row_dot = jnp.sum(weights * along, axis=0, keepdims=True)
        slopes = (weights * (along - row_dot)).astype(jnp.bfloat16)
        key_term = dot(slopes, query_block) * scale
        for half, term in enumerate((key_term, value_term)):
            at = pl.ds(half * LANES, LANES)
            own[g, :, at] = term[:tokens]
            for side in range(2):
                put_side[g, side, pl.ds(0, edge), at] = term[
                    tokens + side * edge : tokens + (side + 1) * edge
                ].astype(jnp.bfloat16)
            for slot in range(slots):
                lat_sum[g, slot, :, at] = term[base + slot * strip : base + (slot + 1) * strip]
                start = base + slots * strip + slot * region
                for side in range(2):
                    first = start + side * (corner - 16)
                    put_side[g, side, pl.ds(edge + slot * corner, corner), at] = term[
                        first : first + corner
                    ].astype(jnp.bfloat16)
        for copy in side_copies(g):
            copy.start()
        attended = dot(value_block.T, probabilities).astype(jnp.bfloat16)
        att_ref[:, lanes] = from_heads(attended.T)
        grad_query = (dot(key_block.T, slopes) * scale).astype(jnp.bfloat16)
        dq_ref[:, lanes] = from_heads(grad_query.T)
        for copy in saves(g, 0):
            copy.start()

    def gather_sides(g):
        for copy in side_copies(g):
            copy.wait_recv()
        low, high = got_side[g, 0], got_side[g, 1]
        own[g] += dot(edge_t_ref[...], jnp.concatenate([low[:edge], high[:edge]], axis=0))
        for slot in range(slots):
            at = edge + slot * corner
            corners = jnp.concatenate([low[at : at + corner], high[at : at + corner]], axis=0)
            total = lat_sum[g, slot] + dot(corner_t_ref[...], corners)
            put_lat[g, slot] = total.astype(jnp.bfloat16)
        for copy in back_copies(g):
            copy.start()

    def finish(g):
        for copy in back_copies(g):
            copy.wait_recv()
        for slot in range(slots):
            own[g, strip_of(slot), :] += got_back[g, slot].astype(jnp.float32)
        dk_ref[:, lanes_of(g)] = own[g, :, pl.ds(0, LANES)].astype(jnp.bfloat16)
        dv_ref[:, lanes_of(g)] = own[g, :, pl.ds(LANES, LANES)].astype(jnp.bfloat16)
        for copy in saves(g, 2):
            copy.start()

    def step(t, carry):
        for delay, stage in enumerate((spread_corners, attend, gather_sides, finish)):
            pl.when((t >= delay) & (t < chunks + delay))(functools.partial(stage, t - delay))
        return carry

    lax.fori_loop(0, chunks + 3, step, 0)

    def drain(g, carry):
        for copy in lat_copies(g) + edge_copies(g) + corner_copies(g) + side_copies(g) + back_copies(g):
            copy.wait_send()
        for copy in saves(g, 0) + saves(g, 2):
            copy.wait()
        return carry

    lax.fori_loop(0, chunks, drain, 0)


def store(a_in, b_in, c_in, d_in, a_out, b_out, c_out, d_out, sem):
    pairs = ((a_in, a_out), (b_in, b_out), (c_in, c_out), (d_in, d_out))
    copies = [pltpu.make_async_copy(src, dst, sem.at[n]) for n, (src, dst) in enumerate(pairs)]
    for copy in copies:
        copy.start()
    for copy in copies:
        copy.wait()


def local(sizes, queries, keys_in, values, grad_out):
    n_lat, n_lon, n_head = sizes
    rows, cols, features = queries.shape
    slots = 1 if n_lat == 2 else 2
    chunks = features // LANES
    tokens, strip, edge = rows * cols, RAD * cols, rows * RAD
    corner = rounded_up(RAD * RAD, 16)
    side = edge + slots * corner
    count = rounded_up(tokens + 2 * edge + slots * (strip + 2 * corner - 16), 128)
    wide = 2 * LANES
    bf16, f32 = jnp.bfloat16, jnp.float32
    hbm = pl.BlockSpec(memory_space=pltpu.HBM)
    flops = 12 * count * tokens * (LANES // HD) * LANES * chunks
    sems = [(4,), (chunks, 4)] + [(chunks, 2 * slots)] * 2 + [(chunks, 2)] * 2 + [(chunks, 2 * slots)] * 2 + [(chunks, 2)] * 2
    sems += [(chunks, slots)] * 2
    out = pl.pallas_call(
        functools.partial(kernel, (rows, cols, slots, n_lat, n_lon, n_head, chunks)),
        out_shape=[jax.ShapeDtypeStruct((tokens, features), bf16)] * 4,
        in_specs=[hbm] * 4,
        out_specs=[hbm] * 4,
        scratch_shapes=[
            *[pltpu.VMEM((tokens, features), bf16)] * 8,
            pltpu.VMEM((2 * edge, tokens), bf16),
            pltpu.VMEM((tokens, 2 * edge), bf16),
            pltpu.VMEM((2 * corner, strip), bf16),
            pltpu.VMEM((strip, 2 * corner), bf16),
            pltpu.VMEM((count, LANES // HD * tokens), f32),
            pltpu.VMEM((count, wide), bf16),
            pltpu.VMEM((chunks, slots, strip, wide), bf16),
            pltpu.VMEM((chunks, 2, edge, wide), bf16),
            pltpu.VMEM((chunks, 2, edge, wide), bf16),
            pltpu.VMEM((chunks, 2 * slots, corner, wide), bf16),
            pltpu.VMEM((chunks, 2 * slots, corner, wide), bf16),
            pltpu.VMEM((chunks, 2, side, wide), bf16),
            pltpu.VMEM((chunks, 2, side, wide), bf16),
            pltpu.VMEM((chunks, slots, strip, wide), bf16),
            pltpu.VMEM((chunks, slots, strip, wide), bf16),
            pltpu.VMEM((chunks, tokens, wide), f32),
            pltpu.VMEM((chunks, slots, strip, wide), f32),
        ]
        + [pltpu.SemaphoreType.DMA(shape) for shape in sems],
        compiler_params=pltpu.CompilerParams(
            collective_id=0, has_side_effects=True, vmem_limit_bytes=64 * 1024 * 1024
        ),
        cost_estimate=pl.CostEstimate(flops=flops, bytes_accessed=8 * tokens * features * 2, transcendentals=0),
    )(
        *(x.reshape(tokens, features) for x in (queries, keys_in, values, grad_out)),
    )
    out = pl.pallas_call(
        store,
        out_shape=[jax.ShapeDtypeStruct((tokens, features), bf16)] * 4,
        in_specs=[hbm] * 4,
        out_specs=[hbm] * 4,
        scratch_shapes=[pltpu.SemaphoreType.DMA((4,))],
        compiler_params=pltpu.CompilerParams(vmem_limit_bytes=64 * 1024 * 1024),
    )(*out)
    return tuple(x.reshape(rows, cols, features) for x in out)


def solution(mesh):
    spec = P("lat", ("lon", "head"), None)
    sizes = tuple(mesh.shape[axis] for axis in ("lat", "lon", "head"))
    return jax.shard_map(
        functools.partial(local, sizes), mesh=mesh, in_specs=(spec,) * 4, out_specs=(spec,) * 4, check_vma=False
    )
```

```python
import functools

import jax
import jax.numpy as jnp
from jax import lax
from jax.experimental import pallas as pl
from jax.experimental.pallas import tpu as pltpu
from jax.sharding import PartitionSpec as P

HD = 64
RAD = 6
LANES = 128
AHEAD = 3
MASKED = -1e30
MESH = pl.DeviceIdType.MESH


def rounded_up(size, step):
    return -(-size // step) * step


def floor_div(i, n):
    return jnp.floor((i + 0.5) * (1.0 / n))


def counted(shape, dim):
    return lax.broadcasted_iota(jnp.int32, shape, dim).astype(jnp.float32)


def edge_token(i, count, cols):
    first = jnp.where(i < count, cols - RAD, 0.0)
    i = jnp.where(i < count, i, i - count)
    row = floor_div(i, RAD)
    return row * cols + (i - row * RAD) + first


def corner_token(i, corner, cols):
    size = RAD * RAD
    lead = corner - size
    token = edge_token(jnp.where(i < corner, i, i - corner - lead + size), size, cols)
    real = (i < size) | (i >= corner + lead)
    return jnp.where(real, token, -1.0)


def key_places(count, rows, cols, strip_row):
    slots = len(strip_row)
    tokens, strip, edge = rows * cols, RAD * cols, rows * RAD
    corner = rounded_up(RAD * RAD, 16)
    region = 2 * corner - 16
    i = counted((count, 1), 0)
    row = floor_div(i, cols)
    col = i - row * cols
    real = jnp.where(i < tokens + 2 * edge + slots * (strip + region), 1.0, 0.0)
    for side in range(2):
        at = i - (tokens + side * edge)
        here = (at >= 0) & (at < edge)
        r = floor_div(at, RAD)
        row = jnp.where(here, r, row)
        col = jnp.where(here, at - r * RAD + (cols if side else -RAD), col)
    base = tokens + 2 * edge
    for slot in range(slots):
        top = jnp.asarray(strip_row[slot], jnp.int32).astype(jnp.float32)
        at = i - (base + slot * strip)
        here = (at >= 0) & (at < strip)
        r = floor_div(at, cols)
        row = jnp.where(here, r + top, row)
        col = jnp.where(here, at - r * cols, col)
        for side in range(2):
            start = base + slots * strip + slot * region
            at = i - (start + side * (region - RAD * RAD))
            here = (at >= 0) & (at < RAD * RAD)
            r = floor_div(at, RAD)
            row = jnp.where(here, r + top, row)
            col = jnp.where(here, at - r * RAD + (cols if side else -RAD), col)
        at = i - (base + slots * strip + slot * region)
        real = jnp.where((at >= RAD * RAD) & (at < region - RAD * RAD), 0.0, real)
    return row, col, real > 0.5


def dot(a, b, a_dim=1, b_dim=0):
    return lax.dot_general(a, b, (((a_dim,), (b_dim,)), ((), ())), preferred_element_type=jnp.float32)


def kernel(
    dims, q_hbm, k_hbm, v_hbm, g_hbm, att_hbm, dq_hbm, dk_hbm, dv_hbm,
    att_ref, dq_ref, dk_ref, dv_ref, q_ref, k_ref, v_ref, g_ref, edge_ref, edge_t_ref, corner_ref, corner_t_ref, bias, keys, got_lat, put_edge, got_edge, put_corner, got_corner, put_side, got_side, put_lat, got_back,
    own, lat_sum, load_sem, save_sem, lat_s, lat_r, edge_s, edge_r, corner_s, corner_r, side_s, side_r, back_s, back_r,
):
    rows, cols, slots, n_lat, n_lon, n_head, chunks = dims
    tokens, strip, edge = rows * cols, RAD * cols, rows * RAD
    corner = rounded_up(RAD * RAD, 16)
    region = 2 * corner - 16
    used = tokens + 2 * edge + slots * (strip + region)
    count = keys.shape[0]
    heads = LANES // HD
    lat, lon, head = lax.axis_index("lat"), lax.axis_index("lon"), lax.axis_index("head")
    column = lon * n_head + head
    ring = n_lon * n_head

    def beside(step):
        c = lax.rem(column + step + ring, ring)
        return (lat, c // n_head, lax.rem(c, n_head))

    right, left = beside(1), beside(-1)
    if slots == 1:
        partners = [(1 - lat, lon, head)]
        first_row = [(1 - lat) * ((rows - RAD) * cols)]
        strip_row = [rows - lat * (rows + RAD)]
        far_slot = [0]
    else:
        partners = [(lax.rem(lat + n_lat - 1, n_lat), lon, head), (lax.rem(lat + 1, n_lat), lon, head)]
        first_row = [0, (rows - RAD) * cols]
        strip_row = [-RAD, rows]
        far_slot = [1, 0]

    def strip_of(slot):
        start = first_row[slot]
        if not isinstance(start, int):
            start = pl.multiple_of(start, 16)
        return pl.ds(start, strip)

    def lanes_of(g):
        return pl.ds(pl.multiple_of(g * LANES, LANES), LANES)

    def remote(src, dst, s, r, device):
        return pltpu.make_async_remote_copy(
            src_ref=src, dst_ref=dst, send_sem=s, recv_sem=r, device_id=device, device_id_type=MESH
        )

    def lat_copies(g):
        made = []
        for slot in range(slots):
            for half, ref in enumerate((k_hbm, v_hbm)):
                made.append(
                    remote(
                        ref.at[strip_of(slot), lanes_of(g)],
                        got_lat.at[g, far_slot[slot], :, pl.ds(half * LANES, LANES)],
                        lat_s.at[g, 2 * slot + half], lat_r.at[g, 2 * far_slot[slot] + half], partners[slot],
                    )
                )
        return made

    def edge_copies(g):
        return [
            remote(put_edge.at[g, side], got_edge.at[g, side], edge_s.at[g, side], edge_r.at[g, side], device)
            for side, device in enumerate((right, left))
        ]

    def corner_copies(g):
        return [
            remote(
                put_corner.at[g, 2 * slot + side], got_corner.at[g, 2 * slot + side],
                corner_s.at[g, 2 * slot + side], corner_r.at[g, 2 * slot + side], device,
            )
            for slot in range(slots)
            for side, device in enumerate((right, left))
        ]

    def side_copies(g):
        return [
            remote(put_side.at[g, side], got_side.at[g, side], side_s.at[g, side], side_r.at[g, side], device)
            for side, device in enumerate((left, right))
        ]

    def back_copies(g):
        return [
            remote(
                put_lat.at[g, slot], got_back.at[g, far_slot[slot]],
                back_s.at[g, slot], back_r.at[g, far_slot[slot]], partners[slot],
            )
            for slot in range(slots)
        ]

    def saves(g, first):
        pairs = ((att_ref, att_hbm), (dq_ref, dq_hbm), (dk_ref, dk_hbm), (dv_ref, dv_hbm))
        return [
            pltpu.make_async_copy(src.at[:, lanes_of(g)], dst.at[:, lanes_of(g)], save_sem.at[g, first + n])
            for n, (src, dst) in enumerate(pairs[first : first + 2])
        ]

    def send_edges(g):
        for half, ref in enumerate((k_ref, v_ref)):
            picked = dot(edge_ref[...], ref[:, lanes_of(g)]).astype(jnp.bfloat16)
            at = pl.ds(half * LANES, LANES)
            put_edge[g, 0, :, at] = picked[:edge]
            put_edge[g, 1, :, at] = picked[edge:]
        for copy in edge_copies(g):
            copy.start()

    loads = [
        pltpu.make_async_copy(src, dst, load_sem.at[n])
        for n, (src, dst) in enumerate(((k_hbm, k_ref), (v_hbm, v_ref), (q_hbm, q_ref), (g_hbm, g_ref)))
    ]
    for load in loads:
        load.start()
    barrier = pltpu.get_barrier_semaphore()
    for device in [left, right] + partners:
        pl.semaphore_signal(barrier, inc=1, device_id=device, device_id_type=MESH)
    pl.semaphore_wait(barrier, 2 + slots)

    def start_lat(g, carry):
        for copy in lat_copies(g):
            copy.start()
        return carry

    ahead = min(AHEAD, chunks)
    lax.fori_loop(0, ahead, start_lat, 0)

    def one_hot(token, place):
        return jnp.where(token == place, 1.0, 0.0).astype(jnp.bfloat16)

    n = 2 * edge
    edge_ref[...] = one_hot(edge_token(counted((n, 1), 0), edge, cols), counted((n, tokens), 1))
    loads[0].wait()
    loads[1].wait()
    for g in range(ahead):
        send_edges(g)
    edge_t_ref[...] = one_hot(edge_token(counted((1, n), 1), edge, cols), counted((tokens, n), 0))
    n = 2 * corner
    corner_ref[...] = one_hot(corner_token(counted((n, 1), 0), corner, cols), counted((n, strip), 1))
    corner_t_ref[...] = one_hot(corner_token(counted((1, n), 1), corner, cols), counted((strip, n), 0))
    key_row, key_col, real = key_places(count, rows, cols, strip_row)
    lat_row = key_row + (lat * rows).astype(jnp.float32)
    valid = real & (lat_row >= 0.0) & (lat_row <= float(rows * n_lat - 1))
    key_row = jnp.where(valid, key_row, 1000.0)
    place = counted((1, heads * tokens), 1)
    place = place - floor_div(place, tokens) * tokens
    place_row = floor_div(place, cols)
    place_col = place - place_row * cols
    near = (jnp.abs(key_row - place_row) <= RAD) & (jnp.abs(key_col - place_col) <= RAD)
    bias[...] = jnp.where(near, 0.0, MASKED)
    if count > used:
        keys[pl.ds(used, count - used), :] = jnp.zeros((count - used, 2 * LANES), jnp.bfloat16)

    loads[2].wait()
    loads[3].wait()
    lane_head = lax.broadcasted_iota(jnp.int32, (tokens, LANES), 1) // HD
    ones = [jnp.where(lane_head == h, 1.0, 0.0).astype(jnp.bfloat16) for h in range(heads)]

    def by_head(block):
        return jnp.concatenate([block * one for one in ones], axis=0)

    def from_heads(stacked):
        total = stacked[:tokens] * ones[0]
        for h in range(1, heads):
            total = total + stacked[h * tokens : (h + 1) * tokens] * ones[h]
        return total

    def spread_corners(g):
        for copy in lat_copies(g):
            copy.wait_recv()
        for slot in range(slots):
            picked = dot(corner_ref[...], got_lat[g, slot]).astype(jnp.bfloat16)
            put_corner[g, 2 * slot] = picked[:corner]
            put_corner[g, 2 * slot + 1] = picked[corner:]
        for copy in corner_copies(g):
            copy.start()

        @pl.when(g + ahead < chunks)
        def _():
            start_lat(g + ahead, 0)
            send_edges(g + ahead)

    def attend(g):
        lanes = lanes_of(g)
        for copy in edge_copies(g) + corner_copies(g):
            copy.wait_recv()
        keys[pl.ds(0, tokens), pl.ds(0, LANES)] = k_ref[:, lanes]
        keys[pl.ds(0, tokens), pl.ds(LANES, LANES)] = v_ref[:, lanes]
        for side in range(2):
            keys[pl.ds(tokens + side * edge, edge), :] = got_edge[g, side]
        base = tokens + 2 * edge
        for slot in range(slots):
            keys[pl.ds(base + slot * strip, strip), :] = got_lat[g, slot]
            start = base + slots * strip + slot * region
            low, high = got_corner[g, 2 * slot], got_corner[g, 2 * slot + 1]
            keys[pl.ds(start, corner - 16), :] = low[: corner - 16]
            keys[pl.ds(start + corner - 16, 16), :] = low[corner - 16 :] + high[:16]
            keys[pl.ds(start + corner, corner - 16), :] = high[16:]
        key_block = keys[:, pl.ds(0, LANES)]
        value_block = keys[:, pl.ds(LANES, LANES)]
        query_block = by_head(q_ref[:, lanes])
        grad_block = by_head(g_ref[:, lanes])
        scale = HD ** -0.5
        scores = dot(key_block, query_block, 1, 1) * scale + bias[...]
        weights = jnp.exp(scores - jnp.max(scores, axis=0, keepdims=True))
        weights = weights * (1.0 / jnp.sum(weights, axis=0, keepdims=True))
        probabilities = weights.astype(jnp.bfloat16)
        value_term = dot(probabilities, grad_block)
        along = dot(value_block, grad_block, 1, 1)
        weights = probabilities.astype(jnp.float32)
        row_dot = jnp.sum(weights * along, axis=0, keepdims=True)
        slopes = (weights * (along - row_dot)).astype(jnp.bfloat16)
        key_term = dot(slopes, query_block) * scale
        for half, term in enumerate((key_term, value_term)):
            at = pl.ds(half * LANES, LANES)
            own[g, :, at] = term[:tokens]
            for side in range(2):
                put_side[g, side, pl.ds(0, edge), at] = term[
                    tokens + side * edge : tokens + (side + 1) * edge
                ].astype(jnp.bfloat16)
            for slot in range(slots):
                lat_sum[g, slot, :, at] = term[base + slot * strip : base + (slot + 1) * strip]
                start = base + slots * strip + slot * region
                for side in range(2):
                    first = start + side * (corner - 16)
                    put_side[g, side, pl.ds(edge + slot * corner, corner), at] = term[
                        first : first + corner
                    ].astype(jnp.bfloat16)
        for copy in side_copies(g):
            copy.start()
        attended = dot(value_block.T, probabilities).astype(jnp.bfloat16)
        att_ref[:, lanes] = from_heads(attended.T)
        grad_query = (dot(key_block.T, slopes) * scale).astype(jnp.bfloat16)
        dq_ref[:, lanes] = from_heads(grad_query.T)
        for copy in saves(g, 0):
            copy.start()

    def gather_sides(g):
        for copy in side_copies(g):
            copy.wait_recv()
        low, high = got_side[g, 0], got_side[g, 1]
        own[g] += dot(edge_t_ref[...], jnp.concatenate([low[:edge], high[:edge]], axis=0))
        for slot in range(slots):
            at = edge + slot * corner
            corners = jnp.concatenate([low[at : at + corner], high[at : at + corner]], axis=0)
            total = lat_sum[g, slot] + dot(corner_t_ref[...], corners)
            put_lat[g, slot] = total.astype(jnp.bfloat16)
        for copy in back_copies(g):
            copy.start()

    def finish(g):
        for copy in back_copies(g):
            copy.wait_recv()
        for slot in range(slots):
            own[g, strip_of(slot), :] += got_back[g, slot].astype(jnp.float32)
        dk_ref[:, lanes_of(g)] = own[g, :, pl.ds(0, LANES)].astype(jnp.bfloat16)
        dv_ref[:, lanes_of(g)] = own[g, :, pl.ds(LANES, LANES)].astype(jnp.bfloat16)
        for copy in saves(g, 2):
            copy.start()

    def step(t, carry):
        for delay, stage in ((0, spread_corners), (1, attend), (3, gather_sides), (5, finish)):
            pl.when((t >= delay) & (t < chunks + delay))(functools.partial(stage, t - delay))
        return carry

    lax.fori_loop(0, chunks + 5, step, 0)

    def drain(g, carry):
        for copy in lat_copies(g) + edge_copies(g) + corner_copies(g) + side_copies(g) + back_copies(g):
            copy.wait_send()
        for copy in saves(g, 0) + saves(g, 2):
            copy.wait()
        return carry

    lax.fori_loop(0, chunks, drain, 0)


def store(a_in, b_in, c_in, d_in, a_out, b_out, c_out, d_out, held, in_sem, out_sem):
    pairs = ((a_in, a_out), (b_in, b_out), (c_in, c_out), (d_in, d_out))
    loads = [pltpu.make_async_copy(src, held.at[n], in_sem.at[n]) for n, (src, _) in enumerate(pairs)]
    saves = [pltpu.make_async_copy(held.at[n], dst, out_sem.at[n]) for n, (_, dst) in enumerate(pairs)]
    for load in loads:
        load.start()
    for load, save in zip(loads, saves):
        load.wait()
        save.start()
    for save in saves:
        save.wait()


def local(sizes, queries, keys_in, values, grad_out):
    n_lat, n_lon, n_head = sizes
    rows, cols, features = queries.shape
    slots = 1 if n_lat == 2 else 2
    chunks = features // LANES
    tokens, strip, edge = rows * cols, RAD * cols, rows * RAD
    corner = rounded_up(RAD * RAD, 16)
    side = edge + slots * corner
    count = rounded_up(tokens + 2 * edge + slots * (strip + 2 * corner - 16), 128)
    wide = 2 * LANES
    bf16, f32 = jnp.bfloat16, jnp.float32
    hbm = pl.BlockSpec(memory_space=pltpu.HBM)
    flops = 12 * count * tokens * (LANES // HD) * LANES * chunks
    sems = [(4,), (chunks, 4)] + [(chunks, 2 * slots)] * 2 + [(chunks, 2)] * 2 + [(chunks, 2 * slots)] * 2 + [(chunks, 2)] * 2
    sems += [(chunks, slots)] * 2
    out = pl.pallas_call(
        functools.partial(kernel, (rows, cols, slots, n_lat, n_lon, n_head, chunks)),
        out_shape=[jax.ShapeDtypeStruct((tokens, features), bf16)] * 4,
        in_specs=[hbm] * 4,
        out_specs=[hbm] * 4,
        scratch_shapes=[
            *[pltpu.VMEM((tokens, features), bf16)] * 8,
            pltpu.VMEM((2 * edge, tokens), bf16),
            pltpu.VMEM((tokens, 2 * edge), bf16),
            pltpu.VMEM((2 * corner, strip), bf16),
            pltpu.VMEM((strip, 2 * corner), bf16),
            pltpu.VMEM((count, LANES // HD * tokens), f32),
            pltpu.VMEM((count, wide), bf16),
            pltpu.VMEM((chunks, slots, strip, wide), bf16),
            pltpu.VMEM((chunks, 2, edge, wide), bf16),
            pltpu.VMEM((chunks, 2, edge, wide), bf16),
            pltpu.VMEM((chunks, 2 * slots, corner, wide), bf16),
            pltpu.VMEM((chunks, 2 * slots, corner, wide), bf16),
            pltpu.VMEM((chunks, 2, side, wide), bf16),
            pltpu.VMEM((chunks, 2, side, wide), bf16),
            pltpu.VMEM((chunks, slots, strip, wide), bf16),
            pltpu.VMEM((chunks, slots, strip, wide), bf16),
            pltpu.VMEM((chunks, tokens, wide), f32),
            pltpu.VMEM((chunks, slots, strip, wide), f32),
        ]
        + [pltpu.SemaphoreType.DMA(shape) for shape in sems],
        compiler_params=pltpu.CompilerParams(
            collective_id=0, has_side_effects=True, vmem_limit_bytes=64 * 1024 * 1024
        ),
        cost_estimate=pl.CostEstimate(flops=flops, bytes_accessed=8 * tokens * features * 2, transcendentals=0),
    )(
        *(x.reshape(tokens, features) for x in (queries, keys_in, values, grad_out)),
    )
    out = pl.pallas_call(
        store,
        out_shape=[jax.ShapeDtypeStruct((tokens, features), bf16)] * 4,
        in_specs=[hbm] * 4,
        out_specs=[hbm] * 4,
        scratch_shapes=[pltpu.VMEM((4, tokens, features), bf16)] + [pltpu.SemaphoreType.DMA((4,))] * 2,
        compiler_params=pltpu.CompilerParams(vmem_limit_bytes=64 * 1024 * 1024),
    )(*out)
    return tuple(x.reshape(rows, cols, features) for x in out)


def solution(mesh):
    spec = P("lat", ("lon", "head"), None)
    sizes = tuple(mesh.shape[axis] for axis in ("lat", "lon", "head"))
    return jax.shard_map(
        functools.partial(local, sizes), mesh=mesh, in_specs=(spec,) * 4, out_specs=(spec,) * 4, check_vma=False
    )
```

```python
import functools

import jax
import jax.numpy as jnp
from jax import lax
from jax.experimental import pallas as pl
from jax.experimental.pallas import tpu as pltpu
from jax.sharding import PartitionSpec as P

HD = 64
RAD = 6
LANES = 256
AHEAD = 2
TILE = 256
MASKED = -1e30
MESH = pl.DeviceIdType.MESH


def rounded_up(size, step):
    return -(-size // step) * step


def floor_div(i, n):
    return jnp.floor((i + 0.5) * (1.0 / n))


def counted(shape, dim):
    return lax.broadcasted_iota(jnp.int32, shape, dim).astype(jnp.float32)


def edge_token(i, count, cols):
    first = jnp.where(i < count, cols - RAD, 0.0)
    i = jnp.where(i < count, i, i - count)
    row = floor_div(i, RAD)
    return row * cols + (i - row * RAD) + first


def corner_token(i, corner, cols):
    size = RAD * RAD
    lead = corner - size
    token = edge_token(jnp.where(i < corner, i, i - corner - lead + size), size, cols)
    real = (i < size) | (i >= corner + lead)
    return jnp.where(real, token, -1.0)


def key_places(count, rows, cols, strip_row):
    slots = len(strip_row)
    tokens, strip, edge = rows * cols, RAD * cols, rows * RAD
    corner = rounded_up(RAD * RAD, 16)
    region = 2 * corner - 16
    i = counted((count, 1), 0)
    row = floor_div(i, cols)
    col = i - row * cols
    real = jnp.where(i < tokens + 2 * edge + slots * (strip + region), 1.0, 0.0)
    for side in range(2):
        at = i - (tokens + side * edge)
        here = (at >= 0) & (at < edge)
        r = floor_div(at, RAD)
        row = jnp.where(here, r, row)
        col = jnp.where(here, at - r * RAD + (cols if side else -RAD), col)
    base = tokens + 2 * edge
    for slot in range(slots):
        top = jnp.asarray(strip_row[slot], jnp.int32).astype(jnp.float32)
        at = i - (base + slot * strip)
        here = (at >= 0) & (at < strip)
        r = floor_div(at, cols)
        row = jnp.where(here, r + top, row)
        col = jnp.where(here, at - r * cols, col)
        for side in range(2):
            start = base + slots * strip + slot * region
            at = i - (start + side * (region - RAD * RAD))
            here = (at >= 0) & (at < RAD * RAD)
            r = floor_div(at, RAD)
            row = jnp.where(here, r + top, row)
            col = jnp.where(here, at - r * RAD + (cols if side else -RAD), col)
        at = i - (base + slots * strip + slot * region)
        real = jnp.where((at >= RAD * RAD) & (at < region - RAD * RAD), 0.0, real)
    return row, col, real > 0.5


def dot(a, b, a_dim=1, b_dim=0):
    return lax.dot_general(a, b, (((a_dim,), (b_dim,)), ((), ())), preferred_element_type=jnp.float32)


def kernel(
    dims, q_hbm, k_hbm, v_hbm, g_hbm, att_hbm, dq_hbm, dk_hbm, dv_hbm,
    att_ref, dq_ref, dk_ref, dv_ref, q_ref, k_ref, v_ref, g_ref, edge_ref, edge_t_ref, corner_ref, corner_t_ref, bias, chances, bends, keys, got_lat, put_edge, got_edge, put_corner, got_corner, put_side, got_side, put_lat, got_back,
    own, lat_sum, load_sem, save_sem, lat_s, lat_r, edge_s, edge_r, corner_s, corner_r, side_s, side_r, back_s, back_r,
):
    rows, cols, slots, n_lat, n_lon, n_head, chunks = dims
    tokens, strip, edge = rows * cols, RAD * cols, rows * RAD
    corner = rounded_up(RAD * RAD, 16)
    region = 2 * corner - 16
    used = tokens + 2 * edge + slots * (strip + region)
    count = keys.shape[0]
    heads = LANES // HD
    lat, lon, head = lax.axis_index("lat"), lax.axis_index("lon"), lax.axis_index("head")
    column = lon * n_head + head
    ring = n_lon * n_head

    def beside(step):
        c = lax.rem(column + step + ring, ring)
        return (lat, c // n_head, lax.rem(c, n_head))

    right, left = beside(1), beside(-1)
    if slots == 1:
        partners = [(1 - lat, lon, head)]
        first_row = [(1 - lat) * ((rows - RAD) * cols)]
        strip_row = [rows - lat * (rows + RAD)]
        far_slot = [0]
    else:
        partners = [(lax.rem(lat + n_lat - 1, n_lat), lon, head), (lax.rem(lat + 1, n_lat), lon, head)]
        first_row = [0, (rows - RAD) * cols]
        strip_row = [-RAD, rows]
        far_slot = [1, 0]

    def strip_of(slot):
        start = first_row[slot]
        if not isinstance(start, int):
            start = pl.multiple_of(start, 16)
        return pl.ds(start, strip)

    def lanes_of(g):
        return pl.ds(pl.multiple_of(g * LANES, LANES), LANES)

    def remote(src, dst, s, r, device):
        return pltpu.make_async_remote_copy(
            src_ref=src, dst_ref=dst, send_sem=s, recv_sem=r, device_id=device, device_id_type=MESH
        )

    def lat_copies(g):
        made = []
        for slot in range(slots):
            for half, ref in enumerate((k_hbm, v_hbm)):
                made.append(
                    remote(
                        ref.at[strip_of(slot), lanes_of(g)],
                        got_lat.at[g, far_slot[slot], :, pl.ds(half * LANES, LANES)],
                        lat_s.at[g, 2 * slot + half], lat_r.at[g, 2 * far_slot[slot] + half], partners[slot],
                    )
                )
        return made

    def edge_copies(g):
        return [
            remote(put_edge.at[g, side], got_edge.at[g, side], edge_s.at[g, side], edge_r.at[g, side], device)
            for side, device in enumerate((right, left))
        ]

    def corner_copies(g):
        return [
            remote(
                put_corner.at[g, 2 * slot + side], got_corner.at[g, 2 * slot + side],
                corner_s.at[g, 2 * slot + side], corner_r.at[g, 2 * slot + side], device,
            )
            for slot in range(slots)
            for side, device in enumerate((right, left))
        ]

    def side_copies(g):
        return [
            remote(put_side.at[g, side], got_side.at[g, side], side_s.at[g, side], side_r.at[g, side], device)
            for side, device in enumerate((left, right))
        ]

    def back_copies(g):
        return [
            remote(
                put_lat.at[g, slot], got_back.at[g, far_slot[slot]],
                back_s.at[g, slot], back_r.at[g, far_slot[slot]], partners[slot],
            )
            for slot in range(slots)
        ]

    def saves(g, first):
        pairs = ((att_ref, att_hbm), (dq_ref, dq_hbm), (dk_ref, dk_hbm), (dv_ref, dv_hbm))
        return [
            pltpu.make_async_copy(src.at[:, lanes_of(g)], dst.at[:, lanes_of(g)], save_sem.at[g, first + n])
            for n, (src, dst) in enumerate(pairs[first : first + 2])
        ]

    def send_edges(g):
        for half, ref in enumerate((k_ref, v_ref)):
            picked = dot(edge_ref[...], ref[:, lanes_of(g)]).astype(jnp.bfloat16)
            at = pl.ds(half * LANES, LANES)
            put_edge[g, 0, :, at] = picked[:edge]
            put_edge[g, 1, :, at] = picked[edge:]
        for copy in edge_copies(g):
            copy.start()

    loads = [
        pltpu.make_async_copy(src, dst, load_sem.at[n])
        for n, (src, dst) in enumerate(((k_hbm, k_ref), (v_hbm, v_ref), (q_hbm, q_ref), (g_hbm, g_ref)))
    ]
    for load in loads:
        load.start()
    barrier = pltpu.get_barrier_semaphore()
    for device in [left, right] + partners:
        pl.semaphore_signal(barrier, inc=1, device_id=device, device_id_type=MESH)
    pl.semaphore_wait(barrier, 2 + slots)

    def start_lat(g, carry):
        for copy in lat_copies(g):
            copy.start()
        return carry

    ahead = min(AHEAD, chunks)
    lax.fori_loop(0, ahead, start_lat, 0)

    def one_hot(token, place):
        return jnp.where(token == place, 1.0, 0.0).astype(jnp.bfloat16)

    n = 2 * edge
    edge_ref[...] = one_hot(edge_token(counted((n, 1), 0), edge, cols), counted((n, tokens), 1))
    loads[0].wait()
    loads[1].wait()
    for g in range(ahead):
        send_edges(g)
    edge_t_ref[...] = one_hot(edge_token(counted((1, n), 1), edge, cols), counted((tokens, n), 0))
    n = 2 * corner
    corner_ref[...] = one_hot(corner_token(counted((n, 1), 0), corner, cols), counted((n, strip), 1))
    corner_t_ref[...] = one_hot(corner_token(counted((1, n), 1), corner, cols), counted((strip, n), 0))
    key_row, key_col, real = key_places(count, rows, cols, strip_row)
    lat_row = key_row + (lat * rows).astype(jnp.float32)
    valid = real & (lat_row >= 0.0) & (lat_row <= float(rows * n_lat - 1))
    key_row = jnp.where(valid, key_row, 1000.0)
    place = counted((1, heads * tokens), 1)
    place = place - floor_div(place, tokens) * tokens
    place_row = floor_div(place, cols)
    place_col = place - place_row * cols
    near = (jnp.abs(key_row - place_row) <= RAD) & (jnp.abs(key_col - place_col) <= RAD)
    bias[...] = jnp.where(near, 0.0, MASKED)
    if count > used:
        keys[pl.ds(used, count - used), :] = jnp.zeros((count - used, 2 * LANES), jnp.bfloat16)

    loads[2].wait()
    loads[3].wait()
    lane_head = lax.broadcasted_iota(jnp.int32, (tokens, LANES), 1) // HD
    ones = [jnp.where(lane_head == h, 1.0, 0.0).astype(jnp.bfloat16) for h in range(heads)]

    def by_head(block):
        return jnp.concatenate([block * one for one in ones], axis=0)

    def from_heads(stacked):
        total = stacked[:tokens] * ones[0]
        for h in range(1, heads):
            total = total + stacked[h * tokens : (h + 1) * tokens] * ones[h]
        return total

    def spread_corners(g):
        for copy in lat_copies(g):
            copy.wait_recv()
        for slot in range(slots):
            picked = dot(corner_ref[...], got_lat[g, slot]).astype(jnp.bfloat16)
            put_corner[g, 2 * slot] = picked[:corner]
            put_corner[g, 2 * slot + 1] = picked[corner:]
        for copy in corner_copies(g):
            copy.start()

        @pl.when(g + ahead < chunks)
        def _():
            start_lat(g + ahead, 0)
            send_edges(g + ahead)

    def attend(g):
        lanes = lanes_of(g)
        for copy in edge_copies(g) + corner_copies(g):
            copy.wait_recv()
        keys[pl.ds(0, tokens), pl.ds(0, LANES)] = k_ref[:, lanes]
        keys[pl.ds(0, tokens), pl.ds(LANES, LANES)] = v_ref[:, lanes]
        for side in range(2):
            keys[pl.ds(tokens + side * edge, edge), :] = got_edge[g, side]
        base = tokens + 2 * edge
        for slot in range(slots):
            keys[pl.ds(base + slot * strip, strip), :] = got_lat[g, slot]
            start = base + slots * strip + slot * region
            low, high = got_corner[g, 2 * slot], got_corner[g, 2 * slot + 1]
            keys[pl.ds(start, corner - 16), :] = low[: corner - 16]
            keys[pl.ds(start + corner - 16, 16), :] = low[corner - 16 :] + high[:16]
            keys[pl.ds(start + corner, corner - 16), :] = high[16:]
        key_block = keys[:, pl.ds(0, LANES)]
        value_block = keys[:, pl.ds(LANES, LANES)]
        query_block = by_head(q_ref[:, lanes])
        grad_block = by_head(g_ref[:, lanes])
        scale = HD ** -0.5
        for first in range(0, heads * tokens, TILE):
            at = pl.ds(first, TILE)
            scores = dot(key_block, query_block[first : first + TILE], 1, 1) * scale + bias[:, at]
            weights = jnp.exp(scores - jnp.max(scores, axis=0, keepdims=True))
            weights = weights * (1.0 / jnp.sum(weights, axis=0, keepdims=True))
            rounded = weights.astype(jnp.bfloat16)
            chances[:, at] = rounded
            along = dot(value_block, grad_block[first : first + TILE], 1, 1)
            weights = rounded.astype(jnp.float32)
            row_dot = jnp.sum(weights * along, axis=0, keepdims=True)
            bends[:, at] = (weights * (along - row_dot)).astype(jnp.bfloat16)
        probabilities, slopes = chances[...], bends[...]
        value_term = dot(probabilities, grad_block)
        key_term = dot(slopes, query_block) * scale
        for half, term in enumerate((key_term, value_term)):
            at = pl.ds(half * LANES, LANES)
            own[g, :, at] = term[:tokens]
            for side in range(2):
                put_side[g, side, pl.ds(0, edge), at] = term[
                    tokens + side * edge : tokens + (side + 1) * edge
                ].astype(jnp.bfloat16)
            for slot in range(slots):
                lat_sum[g, slot, :, at] = term[base + slot * strip : base + (slot + 1) * strip]
                start = base + slots * strip + slot * region
                for side in range(2):
                    first = start + side * (corner - 16)
                    put_side[g, side, pl.ds(edge + slot * corner, corner), at] = term[
                        first : first + corner
                    ].astype(jnp.bfloat16)
        for copy in side_copies(g):
            copy.start()
        attended = dot(value_block.T, probabilities).astype(jnp.bfloat16)
        att_ref[:, lanes] = from_heads(attended.T)
        grad_query = (dot(key_block.T, slopes) * scale).astype(jnp.bfloat16)
        dq_ref[:, lanes] = from_heads(grad_query.T)
        for copy in saves(g, 0):
            copy.start()

    def gather_sides(g):
        for copy in side_copies(g):
            copy.wait_recv()
        low, high = got_side[g, 0], got_side[g, 1]
        own[g] += dot(edge_t_ref[...], jnp.concatenate([low[:edge], high[:edge]], axis=0))
        for slot in range(slots):
            at = edge + slot * corner
            corners = jnp.concatenate([low[at : at + corner], high[at : at + corner]], axis=0)
            total = lat_sum[g, slot] + dot(corner_t_ref[...], corners)
            put_lat[g, slot] = total.astype(jnp.bfloat16)
        for copy in back_copies(g):
            copy.start()

    def finish(g):
        for copy in back_copies(g):
            copy.wait_recv()
        for slot in range(slots):
            own[g, strip_of(slot), :] += got_back[g, slot].astype(jnp.float32)
        dk_ref[:, lanes_of(g)] = own[g, :, pl.ds(0, LANES)].astype(jnp.bfloat16)
        dv_ref[:, lanes_of(g)] = own[g, :, pl.ds(LANES, LANES)].astype(jnp.bfloat16)
        for copy in saves(g, 2):
            copy.start()

    def step(t, carry):
        for delay, stage in ((0, spread_corners), (1, attend), (2, gather_sides), (3, finish)):
            pl.when((t >= delay) & (t < chunks + delay))(functools.partial(stage, t - delay))
        return carry

    lax.fori_loop(0, chunks + 3, step, 0)

    def drain(g, carry):
        for copy in lat_copies(g) + edge_copies(g) + corner_copies(g) + side_copies(g) + back_copies(g):
            copy.wait_send()
        for copy in saves(g, 0) + saves(g, 2):
            copy.wait()
        return carry

    lax.fori_loop(0, chunks, drain, 0)


def store(a_in, b_in, c_in, d_in, a_out, b_out, c_out, d_out, held, in_sem, out_sem):
    pairs = ((a_in, a_out), (b_in, b_out), (c_in, c_out), (d_in, d_out))
    loads = [pltpu.make_async_copy(src, held.at[n], in_sem.at[n]) for n, (src, _) in enumerate(pairs)]
    saves = [pltpu.make_async_copy(held.at[n], dst, out_sem.at[n]) for n, (_, dst) in enumerate(pairs)]
    for load in loads:
        load.start()
    for load, save in zip(loads, saves):
        load.wait()
        save.start()
    for save in saves:
        save.wait()


def local(sizes, queries, keys_in, values, grad_out):
    n_lat, n_lon, n_head = sizes
    rows, cols, features = queries.shape
    slots = 1 if n_lat == 2 else 2
    chunks = features // LANES
    tokens, strip, edge = rows * cols, RAD * cols, rows * RAD
    corner = rounded_up(RAD * RAD, 16)
    side = edge + slots * corner
    count = rounded_up(tokens + 2 * edge + slots * (strip + 2 * corner - 16), 128)
    wide = 2 * LANES
    bf16, f32 = jnp.bfloat16, jnp.float32
    hbm = pl.BlockSpec(memory_space=pltpu.HBM)
    flops = 12 * count * tokens * (LANES // HD) * LANES * chunks
    sems = [(4,), (chunks, 4)] + [(chunks, 2 * slots)] * 2 + [(chunks, 2)] * 2 + [(chunks, 2 * slots)] * 2 + [(chunks, 2)] * 2
    sems += [(chunks, slots)] * 2
    out = pl.pallas_call(
        functools.partial(kernel, (rows, cols, slots, n_lat, n_lon, n_head, chunks)),
        out_shape=[jax.ShapeDtypeStruct((tokens, features), bf16)] * 4,
        in_specs=[hbm] * 4,
        out_specs=[hbm] * 4,
        scratch_shapes=[
            *[pltpu.VMEM((tokens, features), bf16)] * 8,
            pltpu.VMEM((2 * edge, tokens), bf16),
            pltpu.VMEM((tokens, 2 * edge), bf16),
            pltpu.VMEM((2 * corner, strip), bf16),
            pltpu.VMEM((strip, 2 * corner), bf16),
            pltpu.VMEM((count, LANES // HD * tokens), f32),
            pltpu.VMEM((count, LANES // HD * tokens), bf16),
            pltpu.VMEM((count, LANES // HD * tokens), bf16),
            pltpu.VMEM((count, wide), bf16),
            pltpu.VMEM((chunks, slots, strip, wide), bf16),
            pltpu.VMEM((chunks, 2, edge, wide), bf16),
            pltpu.VMEM((chunks, 2, edge, wide), bf16),
            pltpu.VMEM((chunks, 2 * slots, corner, wide), bf16),
            pltpu.VMEM((chunks, 2 * slots, corner, wide), bf16),
            pltpu.VMEM((chunks, 2, side, wide), bf16),
            pltpu.VMEM((chunks, 2, side, wide), bf16),
            pltpu.VMEM((chunks, slots, strip, wide), bf16),
            pltpu.VMEM((chunks, slots, strip, wide), bf16),
            pltpu.VMEM((chunks, tokens, wide), f32),
            pltpu.VMEM((chunks, slots, strip, wide), f32),
        ]
        + [pltpu.SemaphoreType.DMA(shape) for shape in sems],
        compiler_params=pltpu.CompilerParams(
            collective_id=0, has_side_effects=True, vmem_limit_bytes=64 * 1024 * 1024
        ),
        cost_estimate=pl.CostEstimate(flops=flops, bytes_accessed=8 * tokens * features * 2, transcendentals=0),
    )(
        *(x.reshape(tokens, features) for x in (queries, keys_in, values, grad_out)),
    )
    out = pl.pallas_call(
        store,
        out_shape=[jax.ShapeDtypeStruct((tokens, features), bf16)] * 4,
        in_specs=[hbm] * 4,
        out_specs=[hbm] * 4,
        scratch_shapes=[pltpu.VMEM((4, tokens, features), bf16)] + [pltpu.SemaphoreType.DMA((4,))] * 2,
        compiler_params=pltpu.CompilerParams(vmem_limit_bytes=64 * 1024 * 1024),
    )(*out)
    return tuple(x.reshape(rows, cols, features) for x in out)


def solution(mesh):
    spec = P("lat", ("lon", "head"), None)
    sizes = tuple(mesh.shape[axis] for axis in ("lat", "lon", "head"))
    return jax.shard_map(
        functools.partial(local, sizes), mesh=mesh, in_specs=(spec,) * 4, out_specs=(spec,) * 4, check_vma=False
    )
```

```python
import functools

import jax
import jax.numpy as jnp
from jax import lax
from jax.experimental import pallas as pl
from jax.experimental.pallas import tpu as pltpu
from jax.sharding import PartitionSpec as P

HD = 64
RAD = 6
LANES = 256
AHEAD = 2
TILE = 256
MASKED = -1e30
MESH = pl.DeviceIdType.MESH


def rounded_up(size, step):
    return -(-size // step) * step


def floor_div(i, n):
    return jnp.floor((i + 0.5) * (1.0 / n))


def counted(shape, dim):
    return lax.broadcasted_iota(jnp.int32, shape, dim).astype(jnp.float32)


def edge_token(i, count, cols):
    first = jnp.where(i < count, cols - RAD, 0.0)
    i = jnp.where(i < count, i, i - count)
    row = floor_div(i, RAD)
    return row * cols + (i - row * RAD) + first


def corner_token(i, corner, cols):
    size = RAD * RAD
    lead = corner - size
    token = edge_token(jnp.where(i < corner, i, i - corner - lead + size), size, cols)
    real = (i < size) | (i >= corner + lead)
    return jnp.where(real, token, -1.0)


def key_places(count, rows, cols, strip_row):
    slots = len(strip_row)
    tokens, strip, edge = rows * cols, RAD * cols, rows * RAD
    corner = rounded_up(RAD * RAD, 16)
    region = 2 * corner - 16
    i = counted((count, 1), 0)
    row = floor_div(i, cols)
    col = i - row * cols
    real = jnp.where(i < tokens + 2 * edge + slots * (strip + region), 1.0, 0.0)
    for side in range(2):
        at = i - (tokens + side * edge)
        here = (at >= 0) & (at < edge)
        r = floor_div(at, RAD)
        row = jnp.where(here, r, row)
        col = jnp.where(here, at - r * RAD + (cols if side else -RAD), col)
    base = tokens + 2 * edge
    for slot in range(slots):
        top = jnp.asarray(strip_row[slot], jnp.int32).astype(jnp.float32)
        at = i - (base + slot * strip)
        here = (at >= 0) & (at < strip)
        r = floor_div(at, cols)
        row = jnp.where(here, r + top, row)
        col = jnp.where(here, at - r * cols, col)
        for side in range(2):
            start = base + slots * strip + slot * region
            at = i - (start + side * (region - RAD * RAD))
            here = (at >= 0) & (at < RAD * RAD)
            r = floor_div(at, RAD)
            row = jnp.where(here, r + top, row)
            col = jnp.where(here, at - r * RAD + (cols if side else -RAD), col)
        at = i - (base + slots * strip + slot * region)
        real = jnp.where((at >= RAD * RAD) & (at < region - RAD * RAD), 0.0, real)
    return row, col, real > 0.5


def dot(a, b, a_dim=1, b_dim=0):
    return lax.dot_general(a, b, (((a_dim,), (b_dim,)), ((), ())), preferred_element_type=jnp.float32)


def kernel(
    dims, q_hbm, k_hbm, v_hbm, g_hbm, att_hbm, dq_hbm, dk_hbm, dv_hbm,
    att_ref, dq_ref, dk_ref, dv_ref, q_ref, k_ref, v_ref, g_ref, edge_ref, edge_t_ref, corner_ref, corner_t_ref, bias, chances, bends, keys, got_lat, put_edge, got_edge, put_corner, got_corner, put_side, got_side, put_lat, got_back,
    own, lat_sum, load_sem, save_sem, lat_s, lat_r, edge_s, edge_r, corner_s, corner_r, side_s, side_r, back_s, back_r,
):
    rows, cols, slots, n_lat, n_lon, n_head, chunks = dims
    tokens, strip, edge = rows * cols, RAD * cols, rows * RAD
    corner = rounded_up(RAD * RAD, 16)
    region = 2 * corner - 16
    used = tokens + 2 * edge + slots * (strip + region)
    count = keys.shape[0]
    heads = LANES // HD
    lat, lon, head = lax.axis_index("lat"), lax.axis_index("lon"), lax.axis_index("head")
    column = lon * n_head + head
    ring = n_lon * n_head

    def beside(step):
        c = lax.rem(column + step + ring, ring)
        return (lat, c // n_head, lax.rem(c, n_head))

    right, left = beside(1), beside(-1)
    if slots == 1:
        partners = [(1 - lat, lon, head)]
        first_row = [(1 - lat) * ((rows - RAD) * cols)]
        strip_row = [rows - lat * (rows + RAD)]
        far_slot = [0]
    else:
        partners = [(lax.rem(lat + n_lat - 1, n_lat), lon, head), (lax.rem(lat + 1, n_lat), lon, head)]
        first_row = [0, (rows - RAD) * cols]
        strip_row = [-RAD, rows]
        far_slot = [1, 0]

    def strip_of(slot):
        start = first_row[slot]
        if not isinstance(start, int):
            start = pl.multiple_of(start, 16)
        return pl.ds(start, strip)

    def lanes_of(g):
        return pl.ds(pl.multiple_of(g * LANES, LANES), LANES)

    def remote(src, dst, s, r, device):
        return pltpu.make_async_remote_copy(
            src_ref=src, dst_ref=dst, send_sem=s, recv_sem=r, device_id=device, device_id_type=MESH
        )

    def lat_copies(g):
        made = []
        for slot in range(slots):
            for half, ref in enumerate((k_hbm, v_hbm)):
                made.append(
                    remote(
                        ref.at[strip_of(slot), lanes_of(g)],
                        got_lat.at[g, far_slot[slot], :, pl.ds(half * LANES, LANES)],
                        lat_s.at[g, 2 * slot + half], lat_r.at[g, 2 * far_slot[slot] + half], partners[slot],
                    )
                )
        return made

    def edge_copies(g):
        return [
            remote(put_edge.at[g, side], got_edge.at[g, side], edge_s.at[g, side], edge_r.at[g, side], device)
            for side, device in enumerate((right, left))
        ]

    def corner_copies(g):
        return [
            remote(
                put_corner.at[g, 2 * slot + side], got_corner.at[g, 2 * slot + side],
                corner_s.at[g, 2 * slot + side], corner_r.at[g, 2 * slot + side], device,
            )
            for slot in range(slots)
            for side, device in enumerate((right, left))
        ]

    def side_copies(g):
        return [
            remote(put_side.at[g, side], got_side.at[g, side], side_s.at[g, side], side_r.at[g, side], device)
            for side, device in enumerate((left, right))
        ]

    def back_copies(g):
        return [
            remote(
                put_lat.at[g, slot], got_back.at[g, far_slot[slot]],
                back_s.at[g, slot], back_r.at[g, far_slot[slot]], partners[slot],
            )
            for slot in range(slots)
        ]

    def saves(g, first):
        pairs = ((att_ref, att_hbm), (dq_ref, dq_hbm), (dk_ref, dk_hbm), (dv_ref, dv_hbm))
        return [
            pltpu.make_async_copy(src.at[:, lanes_of(g)], dst.at[:, lanes_of(g)], save_sem.at[g, first + n])
            for n, (src, dst) in enumerate(pairs[first : first + 2])
        ]

    def send_edges(g):
        for half, ref in enumerate((k_ref, v_ref)):
            picked = dot(edge_ref[...], ref[:, lanes_of(g)]).astype(jnp.bfloat16)
            at = pl.ds(half * LANES, LANES)
            put_edge[g, 0, :, at] = picked[:edge]
            put_edge[g, 1, :, at] = picked[edge:]
        for copy in edge_copies(g):
            copy.start()

    loads = [
        pltpu.make_async_copy(src, dst, load_sem.at[n])
        for n, (src, dst) in enumerate(((k_hbm, k_ref), (v_hbm, v_ref), (q_hbm, q_ref), (g_hbm, g_ref)))
    ]
    for load in loads:
        load.start()
    barrier = pltpu.get_barrier_semaphore()
    for device in [left, right] + partners:
        pl.semaphore_signal(barrier, inc=1, device_id=device, device_id_type=MESH)
    pl.semaphore_wait(barrier, 2 + slots)

    def start_lat(g, carry):
        for copy in lat_copies(g):
            copy.start()
        return carry

    ahead = min(AHEAD, chunks)
    start_lat(0, 0)

    def one_hot(token, place):
        return jnp.where(token == place, 1.0, 0.0).astype(jnp.bfloat16)

    n = 2 * edge
    edge_ref[...] = one_hot(edge_token(counted((n, 1), 0), edge, cols), counted((n, tokens), 1))
    loads[0].wait()
    loads[1].wait()
    send_edges(0)
    edge_t_ref[...] = one_hot(edge_token(counted((1, n), 1), edge, cols), counted((tokens, n), 0))
    n = 2 * corner
    corner_ref[...] = one_hot(corner_token(counted((n, 1), 0), corner, cols), counted((n, strip), 1))
    corner_t_ref[...] = one_hot(corner_token(counted((1, n), 1), corner, cols), counted((strip, n), 0))
    key_row, key_col, real = key_places(count, rows, cols, strip_row)
    lat_row = key_row + (lat * rows).astype(jnp.float32)
    valid = real & (lat_row >= 0.0) & (lat_row <= float(rows * n_lat - 1))
    key_row = jnp.where(valid, key_row, 1000.0)
    place = counted((1, heads * tokens), 1)
    place = place - floor_div(place, tokens) * tokens
    place_row = floor_div(place, cols)
    place_col = place - place_row * cols
    near = (jnp.abs(key_row - place_row) <= RAD) & (jnp.abs(key_col - place_col) <= RAD)
    bias[...] = jnp.where(near, 0.0, MASKED)
    if count > used:
        keys[pl.ds(used, count - used), :] = jnp.zeros((count - used, 2 * LANES), jnp.bfloat16)

    for g in range(1, ahead):
        start_lat(g, 0)
        send_edges(g)
    loads[2].wait()
    loads[3].wait()
    lane_head = lax.broadcasted_iota(jnp.int32, (tokens, LANES), 1) // HD
    ones = [jnp.where(lane_head == h, 1.0, 0.0).astype(jnp.bfloat16) for h in range(heads)]

    def by_head(block):
        return jnp.concatenate([block * one for one in ones], axis=0)

    def from_heads(stacked):
        total = stacked[:tokens] * ones[0]
        for h in range(1, heads):
            total = total + stacked[h * tokens : (h + 1) * tokens] * ones[h]
        return total

    def spread_corners(g):
        for copy in lat_copies(g):
            copy.wait_recv()
        for slot in range(slots):
            picked = dot(corner_ref[...], got_lat[g, slot]).astype(jnp.bfloat16)
            put_corner[g, 2 * slot] = picked[:corner]
            put_corner[g, 2 * slot + 1] = picked[corner:]
        for copy in corner_copies(g):
            copy.start()

        @pl.when(g + ahead < chunks)
        def _():
            start_lat(g + ahead, 0)
            send_edges(g + ahead)

    def attend(g):
        lanes = lanes_of(g)
        for copy in edge_copies(g) + corner_copies(g):
            copy.wait_recv()
        keys[pl.ds(0, tokens), pl.ds(0, LANES)] = k_ref[:, lanes]
        keys[pl.ds(0, tokens), pl.ds(LANES, LANES)] = v_ref[:, lanes]
        for side in range(2):
            keys[pl.ds(tokens + side * edge, edge), :] = got_edge[g, side]
        base = tokens + 2 * edge
        for slot in range(slots):
            keys[pl.ds(base + slot * strip, strip), :] = got_lat[g, slot]
            start = base + slots * strip + slot * region
            low, high = got_corner[g, 2 * slot], got_corner[g, 2 * slot + 1]
            keys[pl.ds(start, corner - 16), :] = low[: corner - 16]
            keys[pl.ds(start + corner - 16, 16), :] = low[corner - 16 :] + high[:16]
            keys[pl.ds(start + corner, corner - 16), :] = high[16:]
        key_block = keys[:, pl.ds(0, LANES)]
        value_block = keys[:, pl.ds(LANES, LANES)]
        query_block = by_head(q_ref[:, lanes])
        grad_block = by_head(g_ref[:, lanes])
        scale = HD ** -0.5
        for first in range(0, heads * tokens, TILE):
            at = pl.ds(first, TILE)
            scores = dot(key_block, query_block[first : first + TILE], 1, 1) * scale + bias[:, at]
            weights = jnp.exp(scores - jnp.max(scores, axis=0, keepdims=True))
            weights = weights * (1.0 / jnp.sum(weights, axis=0, keepdims=True))
            rounded = weights.astype(jnp.bfloat16)
            chances[:, at] = rounded
            along = dot(value_block, grad_block[first : first + TILE], 1, 1)
            weights = rounded.astype(jnp.float32)
            row_dot = jnp.sum(weights * along, axis=0, keepdims=True)
            bends[:, at] = (weights * (along - row_dot)).astype(jnp.bfloat16)
        probabilities, slopes = chances[...], bends[...]
        value_term = dot(probabilities, grad_block)
        key_term = dot(slopes, query_block) * scale
        for half, term in enumerate((key_term, value_term)):
            at = pl.ds(half * LANES, LANES)
            own[g, :, at] = term[:tokens]
            for side in range(2):
                put_side[g, side, pl.ds(0, edge), at] = term[
                    tokens + side * edge : tokens + (side + 1) * edge
                ].astype(jnp.bfloat16)
            for slot in range(slots):
                lat_sum[g, slot, :, at] = term[base + slot * strip : base + (slot + 1) * strip]
                start = base + slots * strip + slot * region
                for side in range(2):
                    first = start + side * (corner - 16)
                    put_side[g, side, pl.ds(edge + slot * corner, corner), at] = term[
                        first : first + corner
                    ].astype(jnp.bfloat16)
        for copy in side_copies(g):
            copy.start()
        attended = dot(value_block.T, probabilities).astype(jnp.bfloat16)
        att_ref[:, lanes] = from_heads(attended.T)
        grad_query = (dot(key_block.T, slopes) * scale).astype(jnp.bfloat16)
        dq_ref[:, lanes] = from_heads(grad_query.T)
        for copy in saves(g, 0):
            copy.start()

    def gather_sides(g):
        for copy in side_copies(g):
            copy.wait_recv()
        low, high = got_side[g, 0], got_side[g, 1]
        own[g] += dot(edge_t_ref[...], jnp.concatenate([low[:edge], high[:edge]], axis=0))
        for slot in range(slots):
            at = edge + slot * corner
            corners = jnp.concatenate([low[at : at + corner], high[at : at + corner]], axis=0)
            total = lat_sum[g, slot] + dot(corner_t_ref[...], corners)
            put_lat[g, slot] = total.astype(jnp.bfloat16)
        for copy in back_copies(g):
            copy.start()

    def finish(g):
        for copy in back_copies(g):
            copy.wait_recv()
        for slot in range(slots):
            own[g, strip_of(slot), :] += got_back[g, slot].astype(jnp.float32)
        dk_ref[:, lanes_of(g)] = own[g, :, pl.ds(0, LANES)].astype(jnp.bfloat16)
        dv_ref[:, lanes_of(g)] = own[g, :, pl.ds(LANES, LANES)].astype(jnp.bfloat16)
        for copy in saves(g, 2):
            copy.start()

    def step(t, carry):
        for delay, stage in ((0, spread_corners), (1, attend), (2, gather_sides), (3, finish)):
            pl.when((t >= delay) & (t < chunks + delay))(functools.partial(stage, t - delay))
        return carry

    lax.fori_loop(0, chunks + 3, step, 0)

    def drain(g, carry):
        for copy in lat_copies(g) + edge_copies(g) + corner_copies(g) + side_copies(g) + back_copies(g):
            copy.wait_send()
        for copy in saves(g, 0) + saves(g, 2):
            copy.wait()
        return carry

    lax.fori_loop(0, chunks, drain, 0)


def store(a_in, b_in, c_in, d_in, a_out, b_out, c_out, d_out, held, in_sem, out_sem):
    pairs = ((a_in, a_out), (b_in, b_out), (c_in, c_out), (d_in, d_out))
    loads = [pltpu.make_async_copy(src, held.at[n], in_sem.at[n]) for n, (src, _) in enumerate(pairs)]
    saves = [pltpu.make_async_copy(held.at[n], dst, out_sem.at[n]) for n, (_, dst) in enumerate(pairs)]
    for load in loads:
        load.start()
    for load, save in zip(loads, saves):
        load.wait()
        save.start()
    for save in saves:
        save.wait()


def local(sizes, queries, keys_in, values, grad_out):
    n_lat, n_lon, n_head = sizes
    rows, cols, features = queries.shape
    slots = 1 if n_lat == 2 else 2
    chunks = features // LANES
    tokens, strip, edge = rows * cols, RAD * cols, rows * RAD
    corner = rounded_up(RAD * RAD, 16)
    side = edge + slots * corner
    count = rounded_up(tokens + 2 * edge + slots * (strip + 2 * corner - 16), 128)
    wide = 2 * LANES
    bf16, f32 = jnp.bfloat16, jnp.float32
    hbm = pl.BlockSpec(memory_space=pltpu.HBM)
    flops = 12 * count * tokens * (LANES // HD) * LANES * chunks
    sems = [(4,), (chunks, 4)] + [(chunks, 2 * slots)] * 2 + [(chunks, 2)] * 2 + [(chunks, 2 * slots)] * 2 + [(chunks, 2)] * 2
    sems += [(chunks, slots)] * 2
    out = pl.pallas_call(
        functools.partial(kernel, (rows, cols, slots, n_lat, n_lon, n_head, chunks)),
        out_shape=[jax.ShapeDtypeStruct((tokens, features), bf16)] * 4,
        in_specs=[hbm] * 4,
        out_specs=[hbm] * 4,
        scratch_shapes=[
            *[pltpu.VMEM((tokens, features), bf16)] * 8,
            pltpu.VMEM((2 * edge, tokens), bf16),
            pltpu.VMEM((tokens, 2 * edge), bf16),
            pltpu.VMEM((2 * corner, strip), bf16),
            pltpu.VMEM((strip, 2 * corner), bf16),
            pltpu.VMEM((count, LANES // HD * tokens), f32),
            pltpu.VMEM((count, LANES // HD * tokens), bf16),
            pltpu.VMEM((count, LANES // HD * tokens), bf16),
            pltpu.VMEM((count, wide), bf16),
            pltpu.VMEM((chunks, slots, strip, wide), bf16),
            pltpu.VMEM((chunks, 2, edge, wide), bf16),
            pltpu.VMEM((chunks, 2, edge, wide), bf16),
            pltpu.VMEM((chunks, 2 * slots, corner, wide), bf16),
            pltpu.VMEM((chunks, 2 * slots, corner, wide), bf16),
            pltpu.VMEM((chunks, 2, side, wide), bf16),
            pltpu.VMEM((chunks, 2, side, wide), bf16),
            pltpu.VMEM((chunks, slots, strip, wide), bf16),
            pltpu.VMEM((chunks, slots, strip, wide), bf16),
            pltpu.VMEM((chunks, tokens, wide), f32),
            pltpu.VMEM((chunks, slots, strip, wide), f32),
        ]
        + [pltpu.SemaphoreType.DMA(shape) for shape in sems],
        compiler_params=pltpu.CompilerParams(
            collective_id=0, has_side_effects=True, vmem_limit_bytes=64 * 1024 * 1024
        ),
        cost_estimate=pl.CostEstimate(flops=flops, bytes_accessed=8 * tokens * features * 2, transcendentals=0),
    )(
        *(x.reshape(tokens, features) for x in (queries, keys_in, values, grad_out)),
    )
    out = pl.pallas_call(
        store,
        out_shape=[jax.ShapeDtypeStruct((tokens, features), bf16)] * 4,
        in_specs=[hbm] * 4,
        out_specs=[hbm] * 4,
        scratch_shapes=[pltpu.VMEM((4, tokens, features), bf16)] + [pltpu.SemaphoreType.DMA((4,))] * 2,
        compiler_params=pltpu.CompilerParams(vmem_limit_bytes=64 * 1024 * 1024),
    )(*out)
    return tuple(x.reshape(rows, cols, features) for x in out)


def solution(mesh):
    spec = P("lat", ("lon", "head"), None)
    sizes = tuple(mesh.shape[axis] for axis in ("lat", "lon", "head"))
    return jax.shard_map(
        functools.partial(local, sizes), mesh=mesh, in_specs=(spec,) * 4, out_specs=(spec,) * 4, check_vma=False
    )
```
